256 devices in a mesh: vocab: 256 (over z, y, x, core).
Axes of the slice: x: 4, y: 4, z: 8, core: 2. Of those that a mesh axis runs over, the one named last changes fastest.
Arguments:
- embedding_table: bfloat16 [65536, 8192], P('vocab'), may hold values from -6 to 6
- token_ids: int32 [32768], P('vocab'), may hold values from 0 to 65535, as said below
- output_grads: bfloat16 [32768, 8192], P('vocab'), may hold values from -6 to 6
Outputs:
- embedded: bfloat16 [32768, 8192], P('vocab')
- table_grads: bfloat16 [65536, 8192], P('vocab')
The draws below stay inside these ranges and needn't reach their ends.
Inputs may be any that keep to these rules, and one draw needn't show every extreme that they name: `token_ids`: the 128 tokens held by one device have at most 2 ids in any one device's block of consecutive table rows; in every draw one device's block receives exactly 2 ids from the tokens of every device.
All inputs are finite; a program needn't handle non-finite values.
Results may differ from the reference program's by a relative error of at most 0.001.
Values may be sent and summed in bfloat16 or wider, within the bound.
A program may use at most 128 MiB of HBM per device.

```python
import jax
import jax.numpy as jnp

D = 8192
VOCAB = 65536
TOK_DEV = 128
CAP = 2
TOKENS = 32768
N_VOCAB = 256


def draw_token_ids(key, part):
    key = jax.random.fold_in(key, 11)
    key_star, key_device = jax.random.split(key, 2)
    star = jax.random.randint(key_star, (), 0, N_VOCAB).astype(jnp.int32)
    rows_each = VOCAB // N_VOCAB

    def device_ids(index):
        sub = jax.random.fold_in(key_device, index)
        key_slot, key_row, key_order = jax.random.split(sub, 3)
        others = jax.random.permutation(key_slot, (N_VOCAB - 1) * CAP)[:TOK_DEV - CAP].astype(jnp.int32)
        owner_other = (star + 1 + others // CAP) % N_VOCAB
        owners = jnp.concatenate([jnp.full((CAP,), star, jnp.int32), owner_other])
        within = jax.random.randint(key_row, (TOK_DEV,), 0, rows_each).astype(jnp.int32)
        ids = owners * rows_each + within
        return ids[jax.random.permutation(key_order, TOK_DEV)]
    every = jax.vmap(device_ids)(jnp.arange(N_VOCAB, dtype=jnp.int32))
    return every.reshape(TOKENS).astype(jnp.int32)


def levels(key, extent, shards, least, largest):
    def one(position, parts):
        steps = jax.random.uniform(jax.random.fold_in(jax.random.fold_in(key, 6), position), (parts,), jnp.float32, least / len(shards), largest / len(shards))
        return jnp.repeat(jnp.exp(steps), extent[position] // parts).reshape((-1,) + (1,) * (len(extent) - position - 1))

    factor_of = one(*shards[0])
    for cut in shards[1:]:
        factor_of = factor_of * one(*cut)
    return factor_of


def noise(stream_key, extent, width, reach, pieces=(), held_as=jnp.bfloat16):
    gain = levels(stream_key, extent, pieces, -0.22, 0.18) if pieces else 1.0
    entries = jax.random.normal(stream_key, extent, jnp.float32) * width * gain
    return jnp.minimum(jnp.maximum(entries, -reach), reach).astype(held_as)


def setup_inputs(seed: int = 0) -> dict:
    key_list = jax.random.split(jax.random.key(seed), 4)
    return {
        "embedding_table": noise(key_list[0], (VOCAB, D), 1.0, 6.0, ((0, 256),)),
        "token_ids": draw_token_ids(jax.random.fold_in(key_list[3], 71), 0),
        "output_grads": noise(key_list[2], (TOKENS, D), 1.0, 6.0, ((0, 256),)),
    }


def reference(embedding_table, token_ids, output_grads):
    embedded = jnp.take(embedding_table, token_ids, axis=0)
    summed = jax.ops.segment_sum(output_grads.astype(jnp.float32), token_ids, num_segments=VOCAB)
    return embedded, summed.astype(jnp.bfloat16)
```

```python
import jax
import jax.numpy as jnp
from jax import lax
from jax.experimental import pallas as pl
from jax.experimental.pallas import tpu as pltpu
from jax.sharding import PartitionSpec as P

MESH = pl.DeviceIdType.MESH
PLANES = 8
PEERS = 32
ROWS = 256
TOKS = 128
CAP = 2
LANE = 128
POOL = 32
PAIR = PLANES * CAP
CHUNKS = 8
TILE = 512


def ranks_within(owners):
    count = owners.shape[-1]
    earlier = lax.broadcasted_iota(jnp.int32, (count, count), 1) < lax.broadcasted_iota(
        jnp.int32, (count, count), 0
    )
    same = owners[..., :, None] == owners[..., None, :]
    return jnp.sum((same & earlier).astype(jnp.int32), axis=-1)


def general(embedding_table, token_ids, output_grads):
    row_count = embedding_table.shape[0]
    tok_count = token_ids.shape[0]
    width = embedding_table.shape[1]
    devices = lax.axis_size("vocab")
    capacity = 2 * ((tok_count + devices - 1) // devices)
    slots = devices * capacity
    owners = token_ids // row_count
    local_rows = token_ids - owners * row_count
    target = owners * capacity + ranks_within(owners)
    slot_column = lax.broadcasted_iota(jnp.int32, (slots, 1), 0)
    sender = target[None, :] == slot_column
    grad_buffer = jnp.dot(
        sender.astype(jnp.bfloat16), output_grads, preferred_element_type=jnp.float32
    )
    grad_buffer = grad_buffer.astype(jnp.bfloat16).reshape(devices, capacity, width)
    request = jnp.sum(sender.astype(jnp.int32) * (local_rows + 1)[None, :], axis=1)
    received = lax.all_to_all(
        request.reshape(devices, capacity), "vocab", split_axis=0, concat_axis=0, tiled=True
    )
    flat_rows = received.reshape(slots) - 1
    row_iota = lax.broadcasted_iota(jnp.int32, (1, row_count), 1)
    picker = (flat_rows[:, None] == row_iota).astype(jnp.bfloat16)
    picked = jnp.dot(picker, embedding_table, preferred_element_type=jnp.float32)
    picked = picked.astype(jnp.bfloat16).reshape(devices, capacity, width)
    returned = lax.all_to_all(picked, "vocab", split_axis=0, concat_axis=0, tiled=True)
    grads_in = lax.all_to_all(grad_buffer, "vocab", split_axis=0, concat_axis=0, tiled=True)
    slot_row = lax.broadcasted_iota(jnp.int32, (1, slots), 1)
    gatherer = (target[:, None] == slot_row).astype(jnp.bfloat16)
    embedded = jnp.dot(
        gatherer, returned.reshape(slots, width), preferred_element_type=jnp.float32
    ).astype(jnp.bfloat16)
    row_column = lax.broadcasted_iota(jnp.int32, (row_count, 1), 0)
    adder = (row_column == flat_rows[None, :]).astype(jnp.bfloat16)
    table_grads = jnp.dot(
        adder, grads_in.reshape(slots, width), preferred_element_type=jnp.float32
    ).astype(jnp.bfloat16)
    return embedded, table_grads


def iota(shape, axis):
    return lax.broadcasted_iota(jnp.int32, shape, axis)


def ones_where(mask):
    return jnp.where(mask, 1.0, 0.0)


def dot(a, b):
    return jnp.dot(a, b, preferred_element_type=jnp.float32)


def dot_nt(a, b):
    return lax.dot_general(
        a.astype(jnp.bfloat16),
        b.astype(jnp.bfloat16),
        (((1,), (1,)), ((), ())),
        preferred_element_type=jnp.float32,
    )


def kernel(
    ids_ref, table_hbm, grads_hbm, emb_hbm, tgr_hbm, flag_ref,
    table, grads, emb, tgr,
    z_send, g1_recv, e2_recv,
    p_send, e1_recv, g2_recv,
    zreq_send, zreq_recv, preq_send, preq_recv,
    pack, unpack, spread, unspread, pick, adder,
    in_sem, out_sem, req_sem,
    g1_sem, e1_sem, g2_sem, e2_sem,
):
    me = lax.axis_index("vocab")
    z = me // PEERS
    p = lax.rem(me, PEERS)
    width = table.shape[2]

    def z_peer(j):
        return lax.rem(z + j, PLANES)

    def p_peer(j):
        return lax.rem(p + j, PEERS)

    def loop(lo, hi, body):
        def step(j, carry):
            body(j)
            return carry

        lax.fori_loop(lo, hi, step, 0)

    def columns(k):
        return pl.ds(pl.multiple_of(k * width, width), width)

    def grads_in(k):
        return pltpu.make_async_copy(grads_hbm.at[:, columns(k)], grads.at[k], in_sem.at[0, k])

    def table_in(k):
        return pltpu.make_async_copy(table_hbm.at[:, columns(k)], table.at[k], in_sem.at[1, k])

    loop(0, CHUNKS, lambda k: grads_in(k).start())
    loop(0, CHUNKS, lambda k: table_in(k).start())

    barrier = pltpu.get_barrier_semaphore()

    def greet(device):
        pl.semaphore_signal(barrier, inc=1, device_id=(device,), device_id_type=MESH)

    loop(1, PLANES, lambda j: greet(z_peer(j) * PEERS + p))
    loop(1, PEERS, lambda j: greet(z * PEERS + p_peer(j)))

    def z_start(src, dst, send, recv, own):
        def one(j):
            t = z_peer(j)
            pltpu.make_async_remote_copy(
                src_ref=src.at[t], dst_ref=dst.at[z], send_sem=send, recv_sem=recv,
                device_id=(t * PEERS + p,), device_id_type=MESH,
            ).start()

        loop(1, PLANES, one)
        pltpu.make_async_copy(src.at[z], dst.at[z], own).start()

    def p_start(src, dst, send, recv, own):
        def one(j):
            t = p_peer(j)
            pltpu.make_async_remote_copy(
                src_ref=src.at[t], dst_ref=dst.at[p], send_sem=send, recv_sem=recv,
                device_id=(z * PEERS + t,), device_id_type=MESH,
            ).start()

        loop(1, PEERS, one)
        pltpu.make_async_copy(src.at[p], dst.at[p], own).start()

    def wait_bytes(ref, count, sem):
        pltpu.make_async_copy(ref.at[pl.ds(0, count)], ref.at[pl.ds(0, count)], sem).wait()

    def wait_recv(dst, count, recv, own):
        wait_bytes(dst, count - 1, recv)
        wait_bytes(dst, 1, own)

    ids = ids_ref[...]
    plane = lax.shift_right_logical(ids, 13)
    owner = lax.shift_right_logical(ids, 8)
    earlier = iota((TOKS, TOKS), 0) < iota((TOKS, TOKS), 1)

    def rank(key):
        row = jnp.broadcast_to(key.astype(jnp.float32), (TOKS, TOKS))
        return jnp.sum(ones_where((row == row.T) & earlier), axis=0, keepdims=True).astype(jnp.int32)

    place = rank(plane)
    twin = rank(owner)
    late = ones_where(jnp.max(place, axis=1, keepdims=True) >= POOL)
    slot = jnp.where(place < POOL, plane * POOL + place, -1)
    packer = ones_where(iota((PLANES * POOL, TOKS), 0) == slot)
    pack[...] = packer.astype(jnp.bfloat16)
    unpack[...] = packer.T.astype(jnp.bfloat16)
    row_code = ((ids & (ROWS - 1)) + 1).astype(jnp.float32)
    pair_code = ((owner & (PEERS - 1)) * CAP + twin).astype(jnp.float32)
    line = iota((PLANES * 8, TOKS), 0)
    part = line & 7
    fields = jnp.where(part == 0, row_code, jnp.where(part == 1, pair_code, 0.0))
    fields = jnp.where((line >> 3) == plane, fields, 0.0)
    lane_at = jnp.where(place < POOL, lax.rem(z, 4) * POOL + place, -1)
    where_at = ones_where(iota((LANE, TOKS), 0) == lane_at)
    message = dot_nt(fields, where_at) + jnp.where(iota((PLANES * 8, LANE), 0) & 7 == 2, late, 0.0)
    zreq_send[...] = message.reshape(PLANES, 8, LANE)

    pl.semaphore_wait(barrier, PLANES - 1 + PEERS - 1)
    z_start(zreq_send, zreq_recv, req_sem.at[0], req_sem.at[1], req_sem.at[2])

    def pack_grads(k):
        grads_in(k).wait()
        for c in range(0, width, TILE):
            out = dot(pack[...], grads[k, :, c : c + TILE]).astype(jnp.bfloat16)
            z_send[k, :, :, c : c + TILE] = out.reshape(PLANES, POOL, TILE)
        z_start(z_send.at[k], g1_recv.at[k], g1_sem.at[0, k], g1_sem.at[1, k], g1_sem.at[2, k])

    pack_grads(0)

    wait_recv(zreq_recv, PLANES, req_sem.at[1], req_sem.at[2])
    got = zreq_recv[...]
    got = jnp.concatenate([got[:4].sum(axis=0), got[4:].sum(axis=0)], axis=1)
    entries = PLANES * POOL
    entry_row = got[0:1, :]
    entry_pair = got[1:2, :].astype(jnp.int32)
    late = jnp.sum(got[2:3, :], axis=1, keepdims=True)
    valid = entry_row > 0.0
    entry_peer = entry_pair >> 1
    entry_slot = (iota((1, entries), 1) >> 5) * CAP + (entry_pair & 1)
    pair_slot = jnp.where(valid, entry_peer * PAIR + entry_slot, -1)
    line = iota((PEERS * 8, entries), 0)
    fields = jnp.where(((line & 7) == 0) & ((line >> 3) == entry_peer), entry_row, 0.0)
    lane_at = jnp.where(valid, lax.rem(p, 8) * PAIR + entry_slot, -1)
    where_at = ones_where(iota((LANE, entries), 0) == lane_at)
    message = dot_nt(fields, where_at) + jnp.where(iota((PEERS * 8, LANE), 0) & 7 == 2, late, 0.0)
    preq_send[...] = message.reshape(PEERS, 8, LANE)
    p_start(preq_send, preq_recv, req_sem.at[3], req_sem.at[4], req_sem.at[5])
    spreader = ones_where(iota((PEERS * PAIR, entries), 0) == pair_slot)
    spread[...] = spreader.astype(jnp.bfloat16)
    unspread[...] = spreader.T.astype(jnp.bfloat16)

    wait_recv(preq_recv, PEERS, req_sem.at[4], req_sem.at[5])
    got = preq_recv[...]
    got = jnp.concatenate([got[8 * g : 8 * g + 8].sum(axis=0) for g in range(4)], axis=1)
    wanted = got[0:1, :]
    flag_ref[...] = jnp.broadcast_to(jnp.sum(got[2:3, :], axis=1, keepdims=True), flag_ref.shape)
    adding = ones_where((iota((ROWS, PEERS * PAIR), 0) + 1).astype(jnp.float32) == wanted)
    adder[...] = adding.astype(jnp.bfloat16)
    pick[...] = adding.T.astype(jnp.bfloat16)

    def pick_rows(k):
        table_in(k).wait()
        for c in range(0, width, TILE):
            out = dot(pick[...], table[k, :, c : c + TILE]).astype(jnp.bfloat16)
            p_send[k, :, :, c : c + TILE] = out.reshape(PEERS, PAIR, TILE)
        p_start(p_send.at[k], e1_recv.at[k], e1_sem.at[0, k], e1_sem.at[1, k], e1_sem.at[2, k])

    pick_rows(0)

    def first_hop(k):
        pack_grads(k)
        pick_rows(k)

    loop(1, CHUNKS, first_hop)

    def second_hop(k):
        wait_recv(e1_recv.at[k], PEERS, e1_sem.at[1, k], e1_sem.at[2, k])
        wait_bytes(z_send.at[k], PLANES - 1, g1_sem.at[0, k])
        wait_recv(g1_recv.at[k], PLANES, g1_sem.at[1, k], g1_sem.at[2, k])
        for c in range(0, width, TILE):
            rows = e1_recv[k, :, :, c : c + TILE].reshape(PEERS * PAIR, TILE)
            out = dot(unspread[...], rows).astype(jnp.bfloat16)
            z_send[k, :, :, c : c + TILE] = out.reshape(PLANES, POOL, TILE)
        z_start(z_send.at[k], e2_recv.at[k], e2_sem.at[0, k], e2_sem.at[1, k], e2_sem.at[2, k])
        wait_bytes(p_send.at[k], PEERS - 1, e1_sem.at[0, k])
        for c in range(0, width, TILE):
            rows = g1_recv[k, :, :, c : c + TILE].reshape(entries, TILE)
            out = dot(spread[...], rows).astype(jnp.bfloat16)
            p_send[k, :, :, c : c + TILE] = out.reshape(PEERS, PAIR, TILE)
        p_start(p_send.at[k], g2_recv.at[k], g2_sem.at[0, k], g2_sem.at[1, k], g2_sem.at[2, k])

    loop(0, CHUNKS, second_hop)

    def emb_out(k):
        return pltpu.make_async_copy(emb.at[k], emb_hbm.at[:, columns(k)], out_sem.at[0, k])

    def tgr_out(k):
        return pltpu.make_async_copy(tgr.at[k], tgr_hbm.at[:, columns(k)], out_sem.at[1, k])

    def finish(k):
        wait_recv(e2_recv.at[k], PLANES, e2_sem.at[1, k], e2_sem.at[2, k])
        for c in range(0, width, TILE):
            rows = e2_recv[k, :, :, c : c + TILE].reshape(entries, TILE)
            emb[k, :, c : c + TILE] = dot(unpack[...], rows).astype(jnp.bfloat16)
        emb_out(k).start()
        wait_recv(g2_recv.at[k], PEERS, g2_sem.at[1, k], g2_sem.at[2, k])
        for c in range(0, width, TILE):
            rows = g2_recv[k, :, :, c : c + TILE].reshape(PEERS * PAIR, TILE)
            tgr[k, :, c : c + TILE] = dot(adder[...], rows).astype(jnp.bfloat16)
        tgr_out(k).start()

    loop(0, CHUNKS, finish)

    def drain(k):
        emb_out(k).wait()
        tgr_out(k).wait()
        wait_bytes(z_send.at[k], PLANES - 1, e2_sem.at[0, k])
        wait_bytes(p_send.at[k], PEERS - 1, g2_sem.at[0, k])

    loop(0, CHUNKS, drain)
    wait_bytes(zreq_send, PLANES - 1, req_sem.at[0])
    wait_bytes(preq_send, PEERS - 1, req_sem.at[3])


def routed(embedding_table, token_ids, output_grads):
    depth = embedding_table.shape[1]
    width = depth // CHUNKS
    entries, slots = PLANES * POOL, PEERS * PAIR
    bf16, f32 = jnp.bfloat16, jnp.float32
    anywhere = pl.BlockSpec(memory_space=pl.ANY)
    vmem = pl.BlockSpec(memory_space=pltpu.VMEM)
    dma = pltpu.SemaphoreType.DMA
    return pl.pallas_call(
        kernel,
        out_shape=(
            jax.ShapeDtypeStruct((TOKS, depth), bf16),
            jax.ShapeDtypeStruct((ROWS, depth), bf16),
            jax.ShapeDtypeStruct((8, LANE), f32),
        ),
        in_specs=[vmem, anywhere, anywhere],
        out_specs=(anywhere, anywhere, vmem),
        scratch_shapes=[
            pltpu.VMEM((CHUNKS, ROWS, width), bf16),
            pltpu.VMEM((CHUNKS, TOKS, width), bf16),
            pltpu.VMEM((CHUNKS, TOKS, width), bf16),
            pltpu.VMEM((CHUNKS, ROWS, width), bf16),
            pltpu.VMEM((CHUNKS, PLANES, POOL, width), bf16),
            pltpu.VMEM((CHUNKS, PLANES, POOL, width), bf16),
            pltpu.VMEM((CHUNKS, PLANES, POOL, width), bf16),
            pltpu.VMEM((CHUNKS, PEERS, PAIR, width), bf16),
            pltpu.VMEM((CHUNKS, PEERS, PAIR, width), bf16),
            pltpu.VMEM((CHUNKS, PEERS, PAIR, width), bf16),
            pltpu.VMEM((PLANES, 8, LANE), f32),
            pltpu.VMEM((PLANES, 8, LANE), f32),
            pltpu.VMEM((PEERS, 8, LANE), f32),
            pltpu.VMEM((PEERS, 8, LANE), f32),
            pltpu.VMEM((entries, TOKS), bf16),
            pltpu.VMEM((TOKS, entries), bf16),
            pltpu.VMEM((slots, entries), bf16),
            pltpu.VMEM((entries, slots), bf16),
            pltpu.VMEM((slots, ROWS), bf16),
            pltpu.VMEM((ROWS, slots), bf16),
            dma((2, CHUNKS)),
            dma((2, CHUNKS)),
            dma((6,)),
            dma((3, CHUNKS)),
            dma((3, CHUNKS)),
            dma((3, CHUNKS)),
            dma((3, CHUNKS)),
        ],
        compiler_params=pltpu.CompilerParams(
            collective_id=0, has_side_effects=True, vmem_limit_bytes=56 * 1024 * 1024
        ),
    )(token_ids.reshape(1, TOKS), embedding_table, output_grads)


def on_device(embedding_table, token_ids, output_grads):
    embedded, table_grads, late = routed(embedding_table, token_ids, output_grads)

    def again(_):
        emb, tgr = general(embedding_table, token_ids, output_grads)
        return emb, tgr, jnp.float32(0)

    embedded, table_grads, _ = lax.while_loop(
        lambda held: held[2] > 0, again, (embedded, table_grads, late[0, 0])
    )
    return embedded, table_grads


def solution(mesh):
    return jax.shard_map(
        on_device,
        mesh=mesh,
        in_specs=(P("vocab", None), P("vocab"), P("vocab", None)),
        out_specs=(P("vocab", None), P("vocab", None)),
        check_vma=False,
    )
```

```python
import jax
import jax.numpy as jnp
from jax import lax
from jax.experimental import pallas as pl
from jax.experimental.pallas import tpu as pltpu
from jax.sharding import PartitionSpec as P

MESH = pl.DeviceIdType.MESH
PLANES = 8
CHIPS = 16
CORES = 2
ROWS = 256
TOKS = 128
LANE = 128
POOL = 56
STRIDE = 64
PAIR = 48
CHUNKS = 4
ENTRIES = PLANES * STRIDE
SLOTS = CHIPS * PAIR


def ranks_within(owners):
    count = owners.shape[-1]
    earlier = lax.broadcasted_iota(jnp.int32, (count, count), 1) < lax.broadcasted_iota(
        jnp.int32, (count, count), 0
    )
    same = owners[..., :, None] == owners[..., None, :]
    return jnp.sum((same & earlier).astype(jnp.int32), axis=-1)


def general(embedding_table, token_ids, output_grads):
    row_count = embedding_table.shape[0]
    tok_count = token_ids.shape[0]
    width = embedding_table.shape[1]
    devices = lax.axis_size("vocab")
    capacity = 2 * ((tok_count + devices - 1) // devices)
    slots = devices * capacity
    owners = token_ids // row_count
    local_rows = token_ids - owners * row_count
    target = owners * capacity + ranks_within(owners)
    slot_column = lax.broadcasted_iota(jnp.int32, (slots, 1), 0)
    sender = target[None, :] == slot_column
    grad_buffer = jnp.dot(
        sender.astype(jnp.bfloat16), output_grads, preferred_element_type=jnp.float32
    )
    grad_buffer = grad_buffer.astype(jnp.bfloat16).reshape(devices, capacity, width)
    request = jnp.sum(sender.astype(jnp.int32) * (local_rows + 1)[None, :], axis=1)
    received = lax.all_to_all(
        request.reshape(devices, capacity), "vocab", split_axis=0, concat_axis=0, tiled=True
    )
    flat_rows = received.reshape(slots) - 1
    row_iota = lax.broadcasted_iota(jnp.int32, (1, row_count), 1)
    picker = (flat_rows[:, None] == row_iota).astype(jnp.bfloat16)
    picked = jnp.dot(picker, embedding_table, preferred_element_type=jnp.float32)
    picked = picked.astype(jnp.bfloat16).reshape(devices, capacity, width)
    returned = lax.all_to_all(picked, "vocab", split_axis=0, concat_axis=0, tiled=True)
    grads_in = lax.all_to_all(grad_buffer, "vocab", split_axis=0, concat_axis=0, tiled=True)
    slot_row = lax.broadcasted_iota(jnp.int32, (1, slots), 1)
    gatherer = (target[:, None] == slot_row).astype(jnp.bfloat16)
    embedded = jnp.dot(
        gatherer, returned.reshape(slots, width), preferred_element_type=jnp.float32
    ).astype(jnp.bfloat16)
    row_column = lax.broadcasted_iota(jnp.int32, (row_count, 1), 0)
    adder = (row_column == flat_rows[None, :]).astype(jnp.bfloat16)
    table_grads = jnp.dot(
        adder, grads_in.reshape(slots, width), preferred_element_type=jnp.float32
    ).astype(jnp.bfloat16)
    return embedded, table_grads


def iota(shape, axis):
    return lax.broadcasted_iota(jnp.int32, shape, axis)


def ones_where(mask):
    return jnp.where(mask, 1.0, 0.0)


def dot(a, b):
    return jnp.dot(a, b, preferred_element_type=jnp.float32)


def dot_nt(a, b):
    return lax.dot_general(
        a.astype(jnp.bfloat16),
        b.astype(jnp.bfloat16),
        (((1,), (1,)), ((), ())),
        preferred_element_type=jnp.float32,
    )


def kernel(
    ids_ref, table_hbm, grads_hbm, emb_hbm, tgr_hbm, flag_ref,
    table, grads, emb, tgr,
    z_send, g1_recv, e2_recv,
    p_send, e1_recv, g2_recv,
    ids_send, ids_recv, zreq_send, zreq_recv, preq_send, preq_recv, flag_send, flag_recv,
    pack, unpack, spread, unspread, pick, adder,
    in_sem, out_sem, mate_sem, late_sem, req_sem,
    g1_sem, e1_sem, g2_sem, e2_sem,
):
    me = lax.axis_index("vocab")
    core = lax.rem(me, CORES)
    mate = 1 - core
    z = me // (CHIPS * CORES)
    p = lax.rem(me // CORES, CHIPS)
    width = table.shape[3]
    half = width // 2
    bf16 = jnp.bfloat16

    def device(plane, chip, which):
        return ((plane * CHIPS + chip) * CORES + which,)

    def z_peer(j):
        return lax.rem(z + j, PLANES)

    def p_peer(j):
        return lax.rem(p + j, CHIPS)

    def loop(lo, hi, body):
        def step(j, carry):
            body(j)
            return carry

        lax.fori_loop(lo, hi, step, 0)

    def columns(which, k):
        return pl.ds(pl.multiple_of((which * CHUNKS + k) * width, width), width)

    def own_in(hbm, vmem, i, k):
        return pltpu.make_async_copy(hbm.at[:, columns(core, k)], vmem.at[k, core], in_sem.at[i, k])

    def mate_in(hbm, vmem, i, k):
        return pltpu.make_async_remote_copy(
            src_ref=hbm.at[:, columns(mate, k)], dst_ref=vmem.at[k, core],
            send_sem=mate_sem.at[i, k], recv_sem=mate_sem.at[i + 1, k],
            device_id=device(z, p, mate), device_id_type=MESH,
        )

    loop(0, CHUNKS, lambda k: own_in(grads_hbm, grads, 0, k).start())
    loop(0, CHUNKS, lambda k: own_in(table_hbm, table, 1, k).start())

    barrier = pltpu.get_barrier_semaphore()

    def greet(plane, chip, which):
        pl.semaphore_signal(barrier, inc=1, device_id=device(plane, chip, which), device_id_type=MESH)

    greet(z, p, mate)
    loop(1, PLANES, lambda j: greet(z_peer(j), p, core))
    loop(1, CHIPS, lambda j: greet(z, p_peer(j), core))

    def z_start(src, dst, send, recv, own):
        def one(j):
            t = z_peer(j)
            pltpu.make_async_remote_copy(
                src_ref=src.at[t], dst_ref=dst.at[z], send_sem=send, recv_sem=recv,
                device_id=device(t, p, core), device_id_type=MESH,
            ).start()

        loop(1, PLANES, one)
        pltpu.make_async_copy(src.at[z], dst.at[z], own).start()

    def p_start(src, dst, send, recv, own):
        def one(j):
            t = p_peer(j)
            pltpu.make_async_remote_copy(
                src_ref=src.at[t], dst_ref=dst.at[p], send_sem=send, recv_sem=recv,
                device_id=device(z, t, core), device_id_type=MESH,
            ).start()

        loop(1, CHIPS, one)
        pltpu.make_async_copy(src.at[p], dst.at[p], own).start()

    def wait_bytes(ref, count, sem):
        pltpu.make_async_copy(ref.at[pl.ds(0, count)], ref.at[pl.ds(0, count)], sem).wait()

    def wait_recv(dst, count, recv, own):
        wait_bytes(dst, count - 1, recv)
        wait_bytes(dst, 1, own)

    ids_send[...] = jnp.broadcast_to(ids_ref[...], ids_send.shape)
    ids_recv[core] = ids_send[...]
    pl.semaphore_wait(barrier, 1 + PLANES - 1 + CHIPS - 1)
    ids_copy = pltpu.make_async_remote_copy(
        src_ref=ids_send, dst_ref=ids_recv.at[core], send_sem=req_sem.at[0], recv_sem=req_sem.at[1],
        device_id=device(z, p, mate), device_id_type=MESH,
    )
    ids_copy.start()
    loop(0, CHUNKS, lambda k: mate_in(grads_hbm, grads, 0, k).start())
    loop(0, CHUNKS, lambda k: mate_in(table_hbm, table, 2, k).start())
    ids_copy.wait()
    got = ids_recv[...]
    ids = jnp.concatenate([got[0, 0:1], got[1, 0:1]], axis=1)
    toks = CORES * TOKS

    def ranks(keys, kinds, count):
        same = ones_where(iota((kinds, count), 0) == keys)
        earlier = ones_where(iota((count, count), 0) < iota((count, count), 1))
        before = dot(same.astype(bf16), earlier.astype(bf16))
        return jnp.sum(same * before, axis=0, keepdims=True).astype(jnp.int32)

    plane = lax.shift_right_logical(ids, 13)
    owner = lax.shift_right_logical(ids, 8)
    place = ranks(plane, PLANES, toks)
    late = ones_where(jnp.max(place, axis=1, keepdims=True) >= POOL)
    fits = place < POOL
    packer = ones_where(iota((ENTRIES, toks), 0) == jnp.where(fits, plane * STRIDE + place, -1))
    pack[...] = packer.astype(bf16)
    row_code = ((ids & (ROWS - 1)) + 1).astype(jnp.float32)
    owner_code = (owner & (CHIPS * CORES - 1)).astype(jnp.float32)
    line = iota((PLANES * 8, toks), 0)
    part = line & 7
    fields = jnp.where(part == 0, row_code, jnp.where(part == 1, owner_code, 0.0))
    fields = jnp.where((line >> 3) == plane, fields, 0.0)
    lane_at = jnp.where(fits, lax.rem(z, 2) * STRIDE + place, -1)
    where_at = ones_where(iota((LANE, toks), 0) == lane_at)
    message = dot_nt(fields, where_at) + jnp.where(iota((PLANES * 8, LANE), 0) & 7 == 2, late, 0.0)
    zreq_send[...] = message.reshape(PLANES, 8, LANE)
    z_start(zreq_send, zreq_recv, req_sem.at[2], req_sem.at[3], req_sem.at[4])

    def store_z(k, matrix, rows):
        parts = []
        for h in range(2):
            out = dot(matrix, rows[:, h * half : (h + 1) * half])
            parts.append(out.reshape(PLANES, STRIDE, half)[:, :POOL])
        z_send[k] = jnp.concatenate(parts, axis=1).astype(bf16)

    def load_z(ref, k, h):
        rows = ref[k].astype(jnp.float32)[:, h * POOL : (h + 1) * POOL]
        rows = jnp.concatenate([rows, jnp.zeros((PLANES, STRIDE - POOL, half), jnp.float32)], axis=1)
        return rows.reshape(ENTRIES, half).astype(bf16)

    def pack_grads(k):
        own_in(grads_hbm, grads, 0, k).wait()
        mate_in(grads_hbm, grads, 0, k).wait_recv()
        store_z(k, pack[...], grads[k].reshape(toks, width))
        z_start(z_send.at[k], g1_recv.at[k], g1_sem.at[0, k], g1_sem.at[1, k], g1_sem.at[2, k])

    pack_grads(0)
    unpack[...] = packer.T.astype(bf16)

    wait_recv(zreq_recv, PLANES, req_sem.at[3], req_sem.at[4])
    got = zreq_recv[...]
    got = jnp.concatenate([got[2 * g] + got[2 * g + 1] for g in range(PLANES // 2)], axis=1)
    entry_row = got[0:1]
    entry_owner = got[1:2].astype(jnp.int32)
    valid = entry_row > 0.0
    entry_chip = jnp.where(valid, entry_owner >> 1, -1)
    entry_core = (entry_owner & 1).astype(jnp.float32)
    place = ranks(entry_chip, CHIPS, ENTRIES)
    late = jnp.sum(got[2:3], axis=1, keepdims=True)
    late = late + ones_where(jnp.max(place, axis=1, keepdims=True) >= PAIR)
    fits = valid & (place < PAIR)
    line = iota((CHIPS * 8, ENTRIES), 0)
    part = line & 7
    fields = jnp.where(part == 0, entry_row, jnp.where(part == 1, entry_core, 0.0))
    fields = jnp.where((line >> 3) == entry_chip, fields, 0.0)
    lanes = CHIPS // 2 * PAIR
    lane_at = jnp.where(fits, lax.rem(p, CHIPS // 2) * PAIR + place, -1)
    where_at = ones_where(iota((lanes, ENTRIES), 0) == lane_at)
    message = dot_nt(fields, where_at) + jnp.where(iota((CHIPS * 8, lanes), 0) & 7 == 2, late, 0.0)
    preq_send[...] = message.reshape(CHIPS, 8, lanes)
    p_start(preq_send, preq_recv, req_sem.at[5], req_sem.at[6], req_sem.at[7])
    spreader = ones_where(iota((SLOTS, ENTRIES), 0) == jnp.where(fits, entry_chip * PAIR + place, -1))
    spread[...] = spreader.astype(bf16)
    unspread[...] = spreader.T.astype(bf16)

    wait_recv(preq_recv, CHIPS, req_sem.at[6], req_sem.at[7])
    got = preq_recv[...]
    got = jnp.concatenate([got[:8].sum(axis=0), got[8:].sum(axis=0)], axis=1)
    wanted = got[0:1] + got[1:2] * float(ROWS)
    adding = ones_where((iota((CORES * ROWS, SLOTS), 0) + 1).astype(jnp.float32) == wanted)
    adder[...] = adding.astype(bf16)
    pick[...] = adding.T.astype(bf16)
    late = jnp.sum(got[2:3], axis=1, keepdims=True)

    def pick_rows(k):
        own_in(table_hbm, table, 1, k).wait()
        mate_in(table_hbm, table, 2, k).wait_recv()
        rows = table[k].reshape(CORES * ROWS, width)
        for h in range(2):
            at = slice(h * half, (h + 1) * half)
            p_send[k, :, :, at] = dot(pick[...], rows[:, at]).astype(bf16).reshape(CHIPS, PAIR, half)
        p_start(p_send.at[k], e1_recv.at[k], e1_sem.at[0, k], e1_sem.at[1, k], e1_sem.at[2, k])

    pick_rows(0)
    flag_send[...] = jnp.broadcast_to(late, flag_send.shape)
    z_start(flag_send, flag_recv, late_sem.at[0], late_sem.at[1], late_sem.at[2])

    def first_hop(k):
        pack_grads(k)
        pick_rows(k)

    loop(1, CHUNKS, first_hop)

    def second_hop(k):
        wait_recv(e1_recv.at[k], CHIPS, e1_sem.at[1, k], e1_sem.at[2, k])
        wait_bytes(z_send.at[k], PLANES - 1, g1_sem.at[0, k])
        wait_recv(g1_recv.at[k], PLANES, g1_sem.at[1, k], g1_sem.at[2, k])
        store_z(k, unspread[...], e1_recv[k].reshape(SLOTS, width))
        z_start(z_send.at[k], e2_recv.at[k], e2_sem.at[0, k], e2_sem.at[1, k], e2_sem.at[2, k])
        wait_bytes(p_send.at[k], CHIPS - 1, e1_sem.at[0, k])
        for h in range(2):
            out = dot(spread[...], load_z(g1_recv, k, h)).astype(bf16)
            p_send[k, :, :, h * half : (h + 1) * half] = out.reshape(CHIPS, PAIR, half)
        p_start(p_send.at[k], g2_recv.at[k], g2_sem.at[0, k], g2_sem.at[1, k], g2_sem.at[2, k])

    loop(0, CHUNKS, second_hop)

    def own_out(vmem, hbm, i, k):
        return pltpu.make_async_copy(vmem.at[k, core], hbm.at[:, columns(core, k)], out_sem.at[i, k])

    def mate_out(vmem, hbm, i, k):
        return pltpu.make_async_remote_copy(
            src_ref=vmem.at[k, mate], dst_ref=hbm.at[:, columns(core, k)],
            send_sem=mate_sem.at[i, k], recv_sem=mate_sem.at[i + 1, k],
            device_id=device(z, p, mate), device_id_type=MESH,
        )

    def finish(k):
        wait_recv(e2_recv.at[k], PLANES, e2_sem.at[1, k], e2_sem.at[2, k])
        for h in range(2):
            out = dot(unpack[...], load_z(e2_recv, k, h)).astype(bf16)
            emb[k, :, :, h * half : (h + 1) * half] = out.reshape(CORES, TOKS, half)
        mate_out(emb, emb_hbm, 4, k).start()
        own_out(emb, emb_hbm, 0, k).start()
        wait_recv(g2_recv.at[k], CHIPS, g2_sem.at[1, k], g2_sem.at[2, k])
        rows = g2_recv[k].reshape(SLOTS, width)
        for h in range(2):
            out = dot(adder[...], rows[:, h * half : (h + 1) * half]).astype(bf16)
            tgr[k, :, :, h * half : (h + 1) * half] = out.reshape(CORES, ROWS, half)
        mate_out(tgr, tgr_hbm, 6, k).start()
        own_out(tgr, tgr_hbm, 1, k).start()

    loop(0, CHUNKS, finish)
    wait_recv(flag_recv, PLANES, late_sem.at[1], late_sem.at[2])
    flag_ref[0, 0] = jnp.max(flag_recv[...])

    def drain(k):
        mate_in(grads_hbm, grads, 0, k).wait_send()
        mate_in(table_hbm, table, 2, k).wait_send()
        wait_bytes(z_send.at[k], PLANES - 1, e2_sem.at[0, k])
        wait_bytes(p_send.at[k], CHIPS - 1, g2_sem.at[0, k])
        own_out(emb, emb_hbm, 0, k).wait()
        own_out(tgr, tgr_hbm, 1, k).wait()
        mate_out(emb, emb_hbm, 4, k).wait()
        mate_out(tgr, tgr_hbm, 6, k).wait()

    loop(0, CHUNKS, drain)
    wait_bytes(zreq_send, PLANES - 1, req_sem.at[2])
    wait_bytes(preq_send, CHIPS - 1, req_sem.at[5])
    wait_bytes(flag_send, PLANES - 1, late_sem.at[0])


def routed(embedding_table, token_ids, output_grads):
    depth = embedding_table.shape[1]
    width = depth // (CORES * CHUNKS)
    bf16, f32 = jnp.bfloat16, jnp.float32
    anywhere = pl.BlockSpec(memory_space=pl.ANY)
    dma = pltpu.SemaphoreType.DMA
    toks, rows = CORES * TOKS, CORES * ROWS
    z_block = pltpu.VMEM((CHUNKS, PLANES, 2 * POOL, width // 2), bf16)
    p_block = pltpu.VMEM((CHUNKS, CHIPS, PAIR, width), bf16)
    row_block = pltpu.VMEM((CHUNKS, CORES, ROWS, width), bf16)
    tok_block = pltpu.VMEM((CHUNKS, CORES, TOKS, width), bf16)
    z_note = pltpu.VMEM((PLANES, 8, LANE), f32)
    p_note = pltpu.VMEM((CHIPS, 8, CHIPS // 2 * PAIR), f32)
    return pl.pallas_call(
        kernel,
        out_shape=(
            jax.ShapeDtypeStruct((TOKS, depth), bf16),
            jax.ShapeDtypeStruct((ROWS, depth), bf16),
            jax.ShapeDtypeStruct((1, 1), f32),
        ),
        in_specs=[pl.BlockSpec(memory_space=pltpu.VMEM), anywhere, anywhere],
        out_specs=(anywhere, anywhere, pl.BlockSpec(memory_space=pltpu.SMEM)),
        scratch_shapes=[
            row_block, tok_block, tok_block, row_block,
            z_block, z_block, z_block,
            p_block, p_block, p_block,
            pltpu.VMEM((8, TOKS), jnp.int32), pltpu.VMEM((CORES, 8, TOKS), jnp.int32),
            z_note, z_note, p_note, p_note, z_note, z_note,
            pltpu.VMEM((ENTRIES, toks), bf16),
            pltpu.VMEM((toks, ENTRIES), bf16),
            pltpu.VMEM((SLOTS, ENTRIES), bf16),
            pltpu.VMEM((ENTRIES, SLOTS), bf16),
            pltpu.VMEM((SLOTS, rows), bf16),
            pltpu.VMEM((rows, SLOTS), bf16),
            dma((2, CHUNKS)),
            dma((2, CHUNKS)),
            dma((8, CHUNKS)),
            dma((3,)),
            dma((8,)),
            dma((3, CHUNKS)),
            dma((3, CHUNKS)),
            dma((3, CHUNKS)),
            dma((3, CHUNKS)),
        ],
        compiler_params=pltpu.CompilerParams(
            collective_id=0, has_side_effects=True, vmem_limit_bytes=56 * 1024 * 1024
        ),
    )(token_ids.reshape(1, TOKS), embedding_table, output_grads)


def on_device(embedding_table, token_ids, output_grads):
    embedded, table_grads, late = routed(embedding_table, token_ids, output_grads)

    def again(_):
        emb, tgr = general(embedding_table, token_ids, output_grads)
        return emb, tgr, jnp.float32(0)

    embedded, table_grads, _ = lax.while_loop(
        lambda held: held[2] > 0, again, (embedded, table_grads, late[0, 0])
    )
    return embedded, table_grads


def solution(mesh):
    return jax.shard_map(
        on_device,
        mesh=mesh,
        in_specs=(P("vocab", None), P("vocab"), P("vocab", None)),
        out_specs=(P("vocab", None), P("vocab", None)),
        check_vma=False,
    )
```

```python
import jax
import jax.numpy as jnp
from jax import lax
from jax.experimental import pallas as pl
from jax.experimental.pallas import tpu as pltpu
from jax.sharding import PartitionSpec as P

MESH = pl.DeviceIdType.MESH
PLANES = 8
CHIPS = 16
CORES = 2
ROWS = 256
TOKS = 128
LANE = 128
BLOCK = 16
POOL = 48
PASS = 16
PAIR = 48
CHUNKS = 8
LEAD = 3
FIRST = PLANES * POOL
SLOTS = CHIPS * PAIR
SPARE = LANE
ENTRIES = FIRST + SPARE


def ranks_within(owners):
    count = owners.shape[-1]
    earlier = lax.broadcasted_iota(jnp.int32, (count, count), 1) < lax.broadcasted_iota(
        jnp.int32, (count, count), 0
    )
    same = owners[..., :, None] == owners[..., None, :]
    return jnp.sum((same & earlier).astype(jnp.int32), axis=-1)


def general(embedding_table, token_ids, output_grads):
    row_count = embedding_table.shape[0]
    tok_count = token_ids.shape[0]
    width = embedding_table.shape[1]
    devices = lax.axis_size("vocab")
    capacity = 2 * ((tok_count + devices - 1) // devices)
    slots = devices * capacity
    owners = token_ids // row_count
    local_rows = token_ids - owners * row_count
    target = owners * capacity + ranks_within(owners)
    slot_column = lax.broadcasted_iota(jnp.int32, (slots, 1), 0)
    sender = target[None, :] == slot_column
    grad_buffer = jnp.dot(
        sender.astype(jnp.bfloat16), output_grads, preferred_element_type=jnp.float32
    )
    grad_buffer = grad_buffer.astype(jnp.bfloat16).reshape(devices, capacity, width)
    request = jnp.sum(sender.astype(jnp.int32) * (local_rows + 1)[None, :], axis=1)
    received = lax.all_to_all(
        request.reshape(devices, capacity), "vocab", split_axis=0, concat_axis=0, tiled=True
    )
    flat_rows = received.reshape(slots) - 1
    row_iota = lax.broadcasted_iota(jnp.int32, (1, row_count), 1)
    picker = (flat_rows[:, None] == row_iota).astype(jnp.bfloat16)
    picked = jnp.dot(picker, embedding_table, preferred_element_type=jnp.float32)
    picked = picked.astype(jnp.bfloat16).reshape(devices, capacity, width)
    returned = lax.all_to_all(picked, "vocab", split_axis=0, concat_axis=0, tiled=True)
    grads_in = lax.all_to_all(grad_buffer, "vocab", split_axis=0, concat_axis=0, tiled=True)
    slot_row = lax.broadcasted_iota(jnp.int32, (1, slots), 1)
    gatherer = (target[:, None] == slot_row).astype(jnp.bfloat16)
    embedded = jnp.dot(
        gatherer, returned.reshape(slots, width), preferred_element_type=jnp.float32
    ).astype(jnp.bfloat16)
    row_column = lax.broadcasted_iota(jnp.int32, (row_count, 1), 0)
    adder = (row_column == flat_rows[None, :]).astype(jnp.bfloat16)
    table_grads = jnp.dot(
        adder, grads_in.reshape(slots, width), preferred_element_type=jnp.float32
    ).astype(jnp.bfloat16)
    return embedded, table_grads


def iota(shape, axis):
    return lax.broadcasted_iota(jnp.int32, shape, axis)


def ones_where(mask):
    return jnp.where(mask, 1.0, 0.0)


def dot(a, b):
    return jnp.dot(a, b, preferred_element_type=jnp.float32)


def dot_nt(a, b):
    return lax.dot_general(
        a.astype(jnp.bfloat16),
        b.astype(jnp.bfloat16),
        (((1,), (1,)), ((), ())),
        preferred_element_type=jnp.float32,
    )


def kernel(
    ids_ref, table_hbm, grads_hbm, emb_hbm, tgr_hbm, flag_ref,
    table, grads, emb, tgr,
    z_send, g1_recv, e2_recv,
    p_send, e1_recv, g2_recv,
    on_send, back_send,
    ids_send, ids_recv, zreq_send, zreq_recv, preq_send, preq_recv, flag_send, flag_recv,
    onreq_send, onreq_recv,
    pack, unpack, spread, unspread, pick, adder, take, give,
    in_sem, out_sem, mate_sem, late_sem, req_sem, onreq_sem,
    g1_sem, e1_sem, g2_sem, e2_sem, on_sem, back_sem,
):
    me = lax.axis_index("vocab")
    core = lax.rem(me, CORES)
    mate = 1 - core
    z = me // (CHIPS * CORES)
    p = lax.rem(me // CORES, CHIPS)
    width = table.shape[3]
    half = width // 2
    bf16 = jnp.bfloat16
    z_blocks, p_blocks = FIRST // BLOCK, SLOTS // BLOCK

    def device(plane, chip, which):
        return ((plane * CHIPS + chip) * CORES + which,)

    def z_peer(j):
        return lax.rem(z + j, PLANES)

    def p_peer(j):
        return lax.rem(p + j, CHIPS)

    def loop(lo, hi, body):
        def step(j, carry):
            body(j)
            return carry

        lax.fori_loop(lo, hi, step, 0)

    def columns(which, k):
        return pl.ds(pl.multiple_of((which * CHUNKS + k) * width, width), width)

    def own_in(hbm, vmem, i, k):
        return pltpu.make_async_copy(hbm.at[:, columns(core, k)], vmem.at[k, core], in_sem.at[i, k])

    def mate_in(hbm, vmem, i, k):
        return pltpu.make_async_remote_copy(
            src_ref=hbm.at[:, columns(mate, k)], dst_ref=vmem.at[k, core],
            send_sem=mate_sem.at[i, k], recv_sem=mate_sem.at[i + 1, k],
            device_id=device(z, p, mate), device_id_type=MESH,
        )

    loop(0, CHUNKS, lambda k: own_in(grads_hbm, grads, 0, k).start())
    loop(0, CHUNKS, lambda k: own_in(table_hbm, table, 1, k).start())

    def clear(k):
        first = z_blocks + 2
        count = SPARE // BLOCK - 2
        g1_recv[k, pl.ds(first, count)] = jnp.zeros((count, BLOCK, width), bf16)
        first = p_blocks + 2
        e1_recv[k, pl.ds(first, count)] = jnp.zeros((count, BLOCK, width), bf16)

    loop(0, CHUNKS, clear)

    barrier = pltpu.get_barrier_semaphore()

    def greet(plane, chip, which):
        pl.semaphore_signal(barrier, inc=1, device_id=device(plane, chip, which), device_id_type=MESH)

    greet(z, p, mate)
    loop(1, PLANES, lambda j: greet(z_peer(j), p, core))
    loop(1, CHIPS, lambda j: greet(z, p_peer(j), core))

    def z_start(src, dst, send, recv, own, count=1):
        def at(ref, t):
            return ref.at[pl.ds(t * count, count)]

        def one(j):
            t = z_peer(j)
            pltpu.make_async_remote_copy(
                src_ref=at(src, t), dst_ref=at(dst, z), send_sem=send, recv_sem=recv,
                device_id=device(t, p, core), device_id_type=MESH,
            ).start()

        loop(1, PLANES, one)
        pltpu.make_async_copy(at(src, z), at(dst, z), own).start()

    def p_start(src, dst, send, recv, own, count=1):
        def at(ref, t):
            return ref.at[pl.ds(t * count, count)]

        def one(j):
            t = p_peer(j)
            pltpu.make_async_remote_copy(
                src_ref=at(src, t), dst_ref=at(dst, p), send_sem=send, recv_sem=recv,
                device_id=device(z, t, core), device_id_type=MESH,
            ).start()

        loop(1, CHIPS, one)
        pltpu.make_async_copy(at(src, p), at(dst, p), own).start()

    def passed(src, dst, sem, first, side):
        t = lax.rem(z + (1 if side == 0 else PLANES - 1), PLANES)
        return pltpu.make_async_remote_copy(
            src_ref=src.at[side], dst_ref=dst.at[first + side],
            send_sem=sem(side), recv_sem=sem(2 + side),
            device_id=device(t, p, core), device_id_type=MESH,
        )

    def wait_bytes(ref, count, sem):
        pltpu.make_async_copy(ref.at[pl.ds(0, count)], ref.at[pl.ds(0, count)], sem).wait()

    def wait_recv(dst, peers, recv, own, count=1):
        wait_bytes(dst, (peers - 1) * count, recv)
        wait_bytes(dst, count, own)

    ids_send[...] = jnp.broadcast_to(ids_ref[...], ids_send.shape)
    ids_recv[core] = ids_send[...]
    pl.semaphore_wait(barrier, 1 + PLANES - 1 + CHIPS - 1)
    ids_copy = pltpu.make_async_remote_copy(
        src_ref=ids_send, dst_ref=ids_recv.at[core], send_sem=req_sem.at[0], recv_sem=req_sem.at[1],
        device_id=device(z, p, mate), device_id_type=MESH,
    )
    ids_copy.start()
    loop(0, CHUNKS, lambda k: mate_in(grads_hbm, grads, 0, k).start())
    loop(0, CHUNKS, lambda k: mate_in(table_hbm, table, 2, k).start())
    ids_copy.wait()
    got = ids_recv[...]
    ids = jnp.concatenate([got[0, 0:1], got[1, 0:1]], axis=1)
    toks = CORES * TOKS

    def ranks(keys, kinds, count):
        same = ones_where(iota((kinds, count), 0) == keys)
        earlier = ones_where(iota((count, count), 0) < iota((count, count), 1))
        before = dot(same.astype(bf16), earlier.astype(bf16))
        return jnp.sum(same * before, axis=0, keepdims=True).astype(jnp.int32)

    plane = lax.shift_right_logical(ids, 13)
    owner = lax.shift_right_logical(ids, 8)
    place = ranks(plane, PLANES, toks)
    over = place >= POOL
    ahead = (plane - z + PLANES) & (PLANES - 1)
    up = (ahead >= 1) & (ahead <= PLANES // 2)
    mark = jnp.where(over, jnp.where(up, 1, 2), 0)
    there = (plane + jnp.where(over, jnp.where(up, PLANES - 1, 1), 0)) & (PLANES - 1)
    same = ones_where(iota((PLANES, toks), 0) == plane)
    held = jnp.minimum(jnp.sum(same, axis=1, keepdims=True), float(POOL))
    here = ones_where(iota((PLANES, toks), 0) == there)
    held = jnp.sum(here * held, axis=0, keepdims=True).astype(jnp.int32)
    place = jnp.where(over, held + ranks(jnp.where(over, there, -1), PLANES, toks), place)
    plane = there
    late = ones_where(jnp.max(place, axis=1, keepdims=True) >= POOL)
    fits = place < POOL
    packer = ones_where(iota((FIRST, toks), 0) == jnp.where(fits, plane * POOL + place, -1))
    pack[...] = packer.astype(bf16)
    row_code = ((ids & (ROWS - 1)) + 1).astype(jnp.float32)
    owner_code = (owner & (CHIPS * CORES - 1)).astype(jnp.float32)
    line = iota((PLANES * 8, toks), 0)
    part = line & 7
    fields = jnp.where(part == 0, row_code, jnp.where(part == 1, owner_code, 0.0))
    fields = jnp.where(part == 3, mark.astype(jnp.float32), fields)
    fields = jnp.where((line >> 3) == plane, fields, 0.0)
    where_at = ones_where(iota((FIRST, toks), 0) == jnp.where(fits, z * POOL + place, -1))
    message = dot_nt(fields, where_at) + jnp.where(iota((PLANES * 8, FIRST), 0) & 7 == 2, late, 0.0)
    zreq_send[...] = message.reshape(PLANES, 8, FIRST)
    z_start(zreq_send, zreq_recv, req_sem.at[2], req_sem.at[3], req_sem.at[4])

    def store(ref, k, matrix, rows):
        for h in range(2):
            cols = slice(h * half, (h + 1) * half)
            out = dot(matrix, rows[:, cols]).astype(bf16)
            ref[k, :, :, cols] = out.reshape(ref.shape[1], BLOCK, half)

    def pack_grads(k):
        own_in(grads_hbm, grads, 0, k).wait()
        mate_in(grads_hbm, grads, 0, k).wait_recv()
        store(z_send, k, pack[...], grads[k].reshape(toks, width))
        z_start(z_send.at[k], g1_recv.at[k], g1_sem.at[0, k], g1_sem.at[1, k], g1_sem.at[2, k], POOL // BLOCK)


    wait_recv(zreq_recv, PLANES, req_sem.at[3], req_sem.at[4])
    got = zreq_recv[...]
    got = got.sum(axis=0)
    late = jnp.sum(got[2:3], axis=1, keepdims=True)
    mark = got[3:4].astype(jnp.int32)
    turn = ranks(mark - 1, 2, FIRST)
    late = late + ones_where(jnp.max(jnp.where(mark > 0, turn, 0), axis=1, keepdims=True) >= PASS)
    pass_at = jnp.where((mark > 0) & (turn < PASS), (mark - 1) * PASS + turn, -1)
    taker = ones_where(iota((SPARE, FIRST), 0) == pass_at)
    take[...] = taker[: 2 * PASS].astype(bf16)
    message = dot_nt(jnp.concatenate([got[0:2], jnp.zeros((6, FIRST), jnp.float32)], axis=0), taker)
    lane = iota((8, LANE), 1)
    onreq_send[0] = jnp.where(lane < PASS, message, 0.0)
    onreq_send[1] = jnp.where(lane >= PASS, message, 0.0)
    for side in range(2):
        passed(onreq_send, onreq_recv, lambda i: onreq_sem.at[i], 0, side).start()
    got = jnp.where(mark > 0, 0.0, got)
    for side in range(2):
        passed(onreq_send, onreq_recv, lambda i: onreq_sem.at[i], 0, side).wait()
    got = jnp.concatenate([got, onreq_recv[0] + onreq_recv[1]], axis=1)
    entry_row = got[0:1]
    entry_owner = got[1:2].astype(jnp.int32)
    valid = entry_row > 0.0
    entry_chip = jnp.where(valid, entry_owner >> 1, -1)
    entry_core = (entry_owner & 1).astype(jnp.float32)
    place = ranks(entry_chip, CHIPS, ENTRIES)
    late = late + ones_where(jnp.max(place, axis=1, keepdims=True) >= PAIR)
    fits = valid & (place < PAIR)
    line = iota((CHIPS * 8, ENTRIES), 0)
    part = line & 7
    fields = jnp.where(part == 0, entry_row, jnp.where(part == 1, entry_core, 0.0))
    fields = jnp.where((line >> 3) == entry_chip, fields, 0.0)
    lanes = CHIPS // 2 * PAIR
    lane_at = jnp.where(fits, lax.rem(p, CHIPS // 2) * PAIR + place, -1)
    where_at = ones_where(iota((lanes, ENTRIES), 0) == lane_at)
    message = dot_nt(fields, where_at) + jnp.where(iota((CHIPS * 8, lanes), 0) & 7 == 2, late, 0.0)
    preq_send[...] = message.reshape(CHIPS, 8, lanes)
    p_start(preq_send, preq_recv, req_sem.at[5], req_sem.at[6], req_sem.at[7])
    pack_grads(0)
    unpack[...] = packer.T.astype(bf16)
    spreader = ones_where(iota((SLOTS, ENTRIES), 0) == jnp.where(fits, entry_chip * PAIR + place, -1))
    spread[...] = spreader.astype(bf16)
    returned = [taker[PASS : 2 * PASS], taker[:PASS], taker[2 * PASS :]]
    unspread[...] = jnp.concatenate([spreader[:, :FIRST]] + returned, axis=0).T.astype(bf16)
    give[...] = spreader[:, FIRST:].T[: 2 * PASS].astype(bf16)

    wait_recv(preq_recv, CHIPS, req_sem.at[6], req_sem.at[7])
    got = preq_recv[...]
    got = jnp.concatenate([got[:8].sum(axis=0), got[8:].sum(axis=0)], axis=1)
    wanted = got[0:1] + got[1:2] * float(ROWS)
    adding = ones_where((iota((CORES * ROWS, SLOTS), 0) + 1).astype(jnp.float32) == wanted)
    adder[...] = adding.astype(bf16)
    pick[...] = adding.T.astype(bf16)
    late = jnp.sum(got[2:3], axis=1, keepdims=True)

    def pick_rows(k):
        own_in(table_hbm, table, 1, k).wait()
        mate_in(table_hbm, table, 2, k).wait_recv()
        store(p_send, k, pick[...], table[k].reshape(CORES * ROWS, width))
        p_start(p_send.at[k], e1_recv.at[k], e1_sem.at[0, k], e1_sem.at[1, k], e1_sem.at[2, k], PAIR // BLOCK)

    pick_rows(0)
    flag_send[...] = jnp.broadcast_to(late, flag_send.shape)
    z_start(flag_send, flag_recv, late_sem.at[0], late_sem.at[1], late_sem.at[2])

    def first_hop(k):
        pack_grads(k)
        pick_rows(k)

    loop(1, LEAD, first_hop)

    def on(k, side):
        return passed(on_send.at[k], g1_recv.at[k], lambda i: on_sem.at[i, k], z_blocks, side)

    def back(k, side):
        return passed(back_send.at[k], e1_recv.at[k], lambda i: back_sem.at[i, k], p_blocks, side)

    def pass_on(k):
        wait_recv(g1_recv.at[k], PLANES, g1_sem.at[1, k], g1_sem.at[2, k], POOL // BLOCK)
        rows = g1_recv[k, pl.ds(0, z_blocks)].reshape(FIRST, width)
        on_send[k] = dot(take[...], rows).astype(bf16).reshape(2, PASS, width)
        for side in range(2):
            on(k, side).start()
        wait_recv(e1_recv.at[k], CHIPS, e1_sem.at[1, k], e1_sem.at[2, k], PAIR // BLOCK)
        rows = e1_recv[k, pl.ds(0, p_blocks)].reshape(SLOTS, width)
        rows = dot(give[...], rows).astype(bf16).reshape(2, PASS, width)
        back_send[k, 0] = rows[1]
        back_send[k, 1] = rows[0]
        for side in range(2):
            back(k, side).start()

    def second_hop(k):
        wait_bytes(z_send.at[k], (PLANES - 1) * (POOL // BLOCK), g1_sem.at[0, k])
        for side in range(2):
            back(k, side).wait_recv()
        store(z_send, k, unspread[...], e1_recv[k].reshape(SLOTS + SPARE, width))
        z_start(z_send.at[k], e2_recv.at[k], e2_sem.at[0, k], e2_sem.at[1, k], e2_sem.at[2, k], POOL // BLOCK)
        wait_bytes(p_send.at[k], (CHIPS - 1) * (PAIR // BLOCK), e1_sem.at[0, k])
        for side in range(2):
            on(k, side).wait_recv()
        store(p_send, k, spread[...], g1_recv[k].reshape(ENTRIES, width))
        p_start(p_send.at[k], g2_recv.at[k], g2_sem.at[0, k], g2_sem.at[1, k], g2_sem.at[2, k], PAIR // BLOCK)

    def turn_round(k):
        pass_on(k)
        second_hop(k - 1)

    def whole_step(k):
        turn_round(k)
        first_hop(k + LEAD)

    pass_on(0)
    first_hop(LEAD)
    loop(1, CHUNKS - LEAD, whole_step)
    loop(CHUNKS - LEAD, CHUNKS, turn_round)
    second_hop(CHUNKS - 1)

    def own_out(vmem, hbm, i, k):
        return pltpu.make_async_copy(vmem.at[k, core], hbm.at[:, columns(core, k)], out_sem.at[i, k])

    def mate_out(vmem, hbm, i, k):
        return pltpu.make_async_remote_copy(
            src_ref=vmem.at[k, mate], dst_ref=hbm.at[:, columns(core, k)],
            send_sem=mate_sem.at[i, k], recv_sem=mate_sem.at[i + 1, k],
            device_id=device(z, p, mate), device_id_type=MESH,
        )

    def finish(k):
        wait_recv(e2_recv.at[k], PLANES, e2_sem.at[1, k], e2_sem.at[2, k], POOL // BLOCK)
        rows = e2_recv[k].reshape(FIRST, width)
        for h in range(2):
            cols = slice(h * half, (h + 1) * half)
            emb[k, :, :, cols] = dot(unpack[...], rows[:, cols]).astype(bf16).reshape(CORES, TOKS, half)
        mate_out(emb, emb_hbm, 4, k).start()
        own_out(emb, emb_hbm, 0, k).start()
        wait_recv(g2_recv.at[k], CHIPS, g2_sem.at[1, k], g2_sem.at[2, k], PAIR // BLOCK)
        rows = g2_recv[k].reshape(SLOTS, width)
        for h in range(2):
            cols = slice(h * half, (h + 1) * half)
            tgr[k, :, :, cols] = dot(adder[...], rows[:, cols]).astype(bf16).reshape(CORES, ROWS, half)
        mate_out(tgr, tgr_hbm, 6, k).start()
        own_out(tgr, tgr_hbm, 1, k).start()

    loop(0, CHUNKS, finish)
    wait_recv(flag_recv, PLANES, late_sem.at[1], late_sem.at[2])
    flag_ref[0, 0] = jnp.max(flag_recv[...])

    def drain(k):
        mate_in(grads_hbm, grads, 0, k).wait_send()
        mate_in(table_hbm, table, 2, k).wait_send()
        wait_bytes(z_send.at[k], (PLANES - 1) * (POOL // BLOCK), e2_sem.at[0, k])
        wait_bytes(p_send.at[k], (CHIPS - 1) * (PAIR // BLOCK), g2_sem.at[0, k])
        for side in range(2):
            on(k, side).wait_send()
            back(k, side).wait_send()
        own_out(emb, emb_hbm, 0, k).wait()
        own_out(tgr, tgr_hbm, 1, k).wait()
        mate_out(emb, emb_hbm, 4, k).wait()
        mate_out(tgr, tgr_hbm, 6, k).wait()

    loop(0, CHUNKS, drain)
    wait_bytes(zreq_send, PLANES - 1, req_sem.at[2])
    wait_bytes(preq_send, CHIPS - 1, req_sem.at[5])
    wait_bytes(flag_send, PLANES - 1, late_sem.at[0])


def routed(embedding_table, token_ids, output_grads):
    depth = embedding_table.shape[1]
    width = depth // (CORES * CHUNKS)
    bf16, f32 = jnp.bfloat16, jnp.float32
    anywhere = pl.BlockSpec(memory_space=pl.ANY)
    dma = pltpu.SemaphoreType.DMA
    toks, rows = CORES * TOKS, CORES * ROWS

    def blocks(count):
        return pltpu.VMEM((CHUNKS, count // BLOCK, BLOCK, width), bf16)

    row_block = pltpu.VMEM((CHUNKS, CORES, ROWS, width), bf16)
    tok_block = pltpu.VMEM((CHUNKS, CORES, TOKS, width), bf16)
    z_note = pltpu.VMEM((PLANES, 8, FIRST), f32)
    late_note = pltpu.VMEM((PLANES, 8, LANE), f32)
    on_note = pltpu.VMEM((2, 8, LANE), f32)
    p_note = pltpu.VMEM((CHIPS, 8, CHIPS // 2 * PAIR), f32)
    return pl.pallas_call(
        kernel,
        out_shape=(
            jax.ShapeDtypeStruct((TOKS, depth), bf16),
            jax.ShapeDtypeStruct((ROWS, depth), bf16),
            jax.ShapeDtypeStruct((1, 1), f32),
        ),
        in_specs=[pl.BlockSpec(memory_space=pltpu.VMEM), anywhere, anywhere],
        out_specs=(anywhere, anywhere, pl.BlockSpec(memory_space=pltpu.SMEM)),
        scratch_shapes=[
            row_block, tok_block, tok_block, row_block,
            blocks(FIRST), blocks(ENTRIES), blocks(FIRST),
            blocks(SLOTS), blocks(SLOTS + SPARE), blocks(SLOTS),
            blocks(2 * PASS), blocks(2 * PASS),
            pltpu.VMEM((8, TOKS), jnp.int32), pltpu.VMEM((CORES, 8, TOKS), jnp.int32),
            z_note, z_note, p_note, p_note, late_note, late_note,
            on_note, on_note,
            pltpu.VMEM((FIRST, toks), bf16),
            pltpu.VMEM((toks, FIRST), bf16),
            pltpu.VMEM((SLOTS, ENTRIES), bf16),
            pltpu.VMEM((FIRST, SLOTS + SPARE), bf16),
            pltpu.VMEM((SLOTS, rows), bf16),
            pltpu.VMEM((rows, SLOTS), bf16),
            pltpu.VMEM((2 * PASS, FIRST), bf16),
            pltpu.VMEM((2 * PASS, SLOTS), bf16),
            dma((2, CHUNKS)),
            dma((2, CHUNKS)),
            dma((8, CHUNKS)),
            dma((3,)),
            dma((8,)),
            dma((4,)),
            dma((3, CHUNKS)),
            dma((3, CHUNKS)),
            dma((3, CHUNKS)),
            dma((3, CHUNKS)),
            dma((4, CHUNKS)),
            dma((4, CHUNKS)),
        ],
        compiler_params=pltpu.CompilerParams(
            collective_id=0, has_side_effects=True, vmem_limit_bytes=56 * 1024 * 1024
        ),
    )(token_ids.reshape(1, TOKS), embedding_table, output_grads)


def on_device(embedding_table, token_ids, output_grads):
    embedded, table_grads, late = routed(embedding_table, token_ids, output_grads)

    def again(_):
        emb, tgr = general(embedding_table, token_ids, output_grads)
        return emb, tgr, jnp.float32(0)

    embedded, table_grads, _ = lax.while_loop(
        lambda held: held[2] > 0, again, (embedded, table_grads, late[0, 0])
    )
    return embedded, table_grads


def solution(mesh):
    return jax.shard_map(
        on_device,
        mesh=mesh,
        in_specs=(P("vocab", None), P("vocab"), P("vocab", None)),
        out_specs=(P("vocab", None), P("vocab", None)),
        check_vma=False,
    )
```

```python
import jax
import jax.numpy as jnp
from jax import lax
from jax.experimental import pallas as pl
from jax.experimental.pallas import tpu as pltpu
from jax.sharding import PartitionSpec as P

MESH = pl.DeviceIdType.MESH
PLANES = 8
CHIPS = 16
CORES = 2
ROWS = 256
TOKS = 128
LANE = 128
BLOCK = 16
POOL = 48
PASS = 16
PAIR = 48
CHUNKS = 8
LEAD = 3
FIRST = PLANES * POOL
SLOTS = CHIPS * PAIR
SPARE = LANE
ENTRIES = FIRST + SPARE


def ranks_within(owners):
    count = owners.shape[-1]
    earlier = lax.broadcasted_iota(jnp.int32, (count, count), 1) < lax.broadcasted_iota(
        jnp.int32, (count, count), 0
    )
    same = owners[..., :, None] == owners[..., None, :]
    return jnp.sum((same & earlier).astype(jnp.int32), axis=-1)


def general(embedding_table, token_ids, output_grads):
    row_count = embedding_table.shape[0]
    tok_count = token_ids.shape[0]
    width = embedding_table.shape[1]
    devices = lax.axis_size("vocab")
    capacity = 2 * ((tok_count + devices - 1) // devices)
    slots = devices * capacity
    owners = token_ids // row_count
    local_rows = token_ids - owners * row_count
    target = owners * capacity + ranks_within(owners)
    slot_column = lax.broadcasted_iota(jnp.int32, (slots, 1), 0)
    sender = target[None, :] == slot_column
    grad_buffer = jnp.dot(
        sender.astype(jnp.bfloat16), output_grads, preferred_element_type=jnp.float32
    )
    grad_buffer = grad_buffer.astype(jnp.bfloat16).reshape(devices, capacity, width)
    request = jnp.sum(sender.astype(jnp.int32) * (local_rows + 1)[None, :], axis=1)
    received = lax.all_to_all(
        request.reshape(devices, capacity), "vocab", split_axis=0, concat_axis=0, tiled=True
    )
    flat_rows = received.reshape(slots) - 1
    row_iota = lax.broadcasted_iota(jnp.int32, (1, row_count), 1)
    picker = (flat_rows[:, None] == row_iota).astype(jnp.bfloat16)
    picked = jnp.dot(picker, embedding_table, preferred_element_type=jnp.float32)
    picked = picked.astype(jnp.bfloat16).reshape(devices, capacity, width)
    returned = lax.all_to_all(picked, "vocab", split_axis=0, concat_axis=0, tiled=True)
    grads_in = lax.all_to_all(grad_buffer, "vocab", split_axis=0, concat_axis=0, tiled=True)
    slot_row = lax.broadcasted_iota(jnp.int32, (1, slots), 1)
    gatherer = (target[:, None] == slot_row).astype(jnp.bfloat16)
    embedded = jnp.dot(
        gatherer, returned.reshape(slots, width), preferred_element_type=jnp.float32
    ).astype(jnp.bfloat16)
    row_column = lax.broadcasted_iota(jnp.int32, (row_count, 1), 0)
    adder = (row_column == flat_rows[None, :]).astype(jnp.bfloat16)
    table_grads = jnp.dot(
        adder, grads_in.reshape(slots, width), preferred_element_type=jnp.float32
    ).astype(jnp.bfloat16)
    return embedded, table_grads


def iota(shape, axis):
    return lax.broadcasted_iota(jnp.int32, shape, axis)


def ones_where(mask):
    return jnp.where(mask, 1.0, 0.0)


def dot(a, b):
    return jnp.dot(a, b, preferred_element_type=jnp.float32)


def dot_nt(a, b):
    return lax.dot_general(
        a.astype(jnp.bfloat16),
        b.astype(jnp.bfloat16),
        (((1,), (1,)), ((), ())),
        preferred_element_type=jnp.float32,
    )


def kernel(
    ids_ref, table_hbm, grads_hbm, emb_hbm, tgr_hbm, flag_ref,
    table, grads, emb, tgr,
    z_send, g1_recv, e2_recv,
    p_send, e1_recv, g2_recv,
    on_send, back_send,
    ids_send, line_recv, preq_send, preq_recv, flag_send, flag_recv,
    pack, unpack, spread, unspread, pick, adder, take, give,
    in_sem, out_sem, mate_sem, late_sem, req_sem,
    g1_sem, e1_sem, g2_sem, e2_sem, on_sem, back_sem,
):
    me = lax.axis_index("vocab")
    core = lax.rem(me, CORES)
    mate = 1 - core
    z = me // (CHIPS * CORES)
    p = lax.rem(me // CORES, CHIPS)
    width = table.shape[3]
    half = width // 2
    bf16 = jnp.bfloat16
    z_blocks, p_blocks = FIRST // BLOCK, SLOTS // BLOCK

    def device(plane, chip, which):
        return ((plane * CHIPS + chip) * CORES + which,)

    def z_peer(j):
        return lax.rem(z + j, PLANES)

    def p_peer(j):
        return lax.rem(p + j, CHIPS)

    def loop(lo, hi, body):
        def step(j, carry):
            body(j)
            return carry

        lax.fori_loop(lo, hi, step, 0)

    def columns(which, k):
        return pl.ds(pl.multiple_of((which * CHUNKS + k) * width, width), width)

    def own_in(hbm, vmem, i, k):
        return pltpu.make_async_copy(hbm.at[:, columns(core, k)], vmem.at[k, core], in_sem.at[i, k])

    def mate_in(hbm, vmem, i, k):
        return pltpu.make_async_remote_copy(
            src_ref=hbm.at[:, columns(mate, k)], dst_ref=vmem.at[k, core],
            send_sem=mate_sem.at[i, k], recv_sem=mate_sem.at[i + 1, k],
            device_id=device(z, p, mate), device_id_type=MESH,
        )

    loop(0, CHUNKS, lambda k: own_in(grads_hbm, grads, 0, k).start())
    loop(0, CHUNKS, lambda k: own_in(table_hbm, table, 1, k).start())

    def clear(k):
        first = z_blocks + 2
        count = SPARE // BLOCK - 2
        g1_recv[k, pl.ds(first, count)] = jnp.zeros((count, BLOCK, width), bf16)
        first = p_blocks + 2
        e1_recv[k, pl.ds(first, count)] = jnp.zeros((count, BLOCK, width), bf16)

    loop(0, CHUNKS, clear)

    barrier = pltpu.get_barrier_semaphore()

    def greet(plane, chip, which):
        pl.semaphore_signal(barrier, inc=1, device_id=device(plane, chip, which), device_id_type=MESH)

    line_count = PLANES * CORES
    line_me = z * CORES + core

    def line_peer(j):
        return lax.rem(line_me + j, line_count)

    loop(1, line_count, lambda j: greet(line_peer(j) // CORES, p, lax.rem(line_peer(j), CORES)))
    loop(1, CHIPS, lambda j: greet(z, p_peer(j), core))

    def z_start(src, dst, send, recv, own, count=1):
        def at(ref, t):
            return ref.at[pl.ds(t * count, count)]

        def one(j):
            t = z_peer(j)
            pltpu.make_async_remote_copy(
                src_ref=at(src, t), dst_ref=at(dst, z), send_sem=send, recv_sem=recv,
                device_id=device(t, p, core), device_id_type=MESH,
            ).start()

        loop(1, PLANES, one)
        pltpu.make_async_copy(at(src, z), at(dst, z), own).start()

    def p_start(src, dst, send, recv, own, count=1):
        def at(ref, t):
            return ref.at[pl.ds(t * count, count)]

        def one(j):
            t = p_peer(j)
            pltpu.make_async_remote_copy(
                src_ref=at(src, t), dst_ref=at(dst, p), send_sem=send, recv_sem=recv,
                device_id=device(z, t, core), device_id_type=MESH,
            ).start()

        loop(1, CHIPS, one)
        pltpu.make_async_copy(at(src, p), at(dst, p), own).start()

    def passed(src, dst, sem, first, side):
        t = lax.rem(z + (1 if side == 0 else PLANES - 1), PLANES)
        return pltpu.make_async_remote_copy(
            src_ref=src.at[side], dst_ref=dst.at[first + side],
            send_sem=sem(side), recv_sem=sem(2 + side),
            device_id=device(t, p, core), device_id_type=MESH,
        )

    def wait_bytes(ref, count, sem):
        pltpu.make_async_copy(ref.at[pl.ds(0, count)], ref.at[pl.ds(0, count)], sem).wait()

    def wait_recv(dst, peers, recv, own, count=1):
        wait_bytes(dst, (peers - 1) * count, recv)
        wait_bytes(dst, count, own)

    ids_send[...] = jnp.broadcast_to(ids_ref[...], ids_send.shape)
    line_recv[line_me] = ids_send[...]
    pl.semaphore_wait(barrier, line_count - 1 + CHIPS - 1)

    def ids_copy(j):
        t = line_peer(j)
        return pltpu.make_async_remote_copy(
            src_ref=ids_send, dst_ref=line_recv.at[line_me],
            send_sem=req_sem.at[0], recv_sem=req_sem.at[1],
            device_id=device(t // CORES, p, lax.rem(t, CORES)), device_id_type=MESH,
        )

    loop(1, line_count, lambda j: ids_copy(j).start())
    loop(0, CHUNKS, lambda k: mate_in(grads_hbm, grads, 0, k).start())
    loop(0, CHUNKS, lambda k: mate_in(table_hbm, table, 2, k).start())
    wait_bytes(line_recv, line_count - 1, req_sem.at[1])
    toks = CORES * TOKS
    got = line_recv[...].reshape(PLANES, CORES, 8, TOKS)
    ids = jnp.concatenate([got[:, c].reshape(PLANES * 8, TOKS) for c in range(CORES)], axis=1)

    def ranks(keys, kinds, count):
        same = ones_where(iota((kinds, count), 0) == keys)
        earlier = ones_where(iota((count, count), 0) < iota((count, count), 1))
        before = dot(same.astype(bf16), earlier.astype(bf16))
        return jnp.sum(same * before, axis=0, keepdims=True).astype(jnp.int32)

    shape = (PLANES * 8, toks)
    chip = iota(shape, 0) >> 3
    part = iota(shape, 0) & 7
    earlier = ones_where(iota((toks, toks), 0) < iota((toks, toks), 1)).astype(bf16)

    def before(mask):
        return dot(mask.astype(bf16), earlier)

    def over_parts(x):
        x = jnp.sum(x.reshape(PLANES, 8, toks), axis=1, keepdims=True)
        return jnp.broadcast_to(x, (PLANES, 8, toks)).reshape(shape).astype(jnp.int32)

    plane = lax.shift_right_logical(ids, 13)
    owner = lax.shift_right_logical(ids, 8)
    same = ones_where(plane == part)
    place = over_parts(same * before(same))
    over = place >= POOL
    ahead = (plane - chip + PLANES) & (PLANES - 1)
    up = (ahead >= 1) & (ahead <= PLANES // 2)
    mark = jnp.where(over, jnp.where(up, 1, 2), 0)
    there = (plane + jnp.where(over, jnp.where(up, PLANES - 1, 1), 0)) & (PLANES - 1)
    held = jnp.minimum(jnp.sum(same, axis=1, keepdims=True), float(POOL))
    here = ones_where(there == part)
    moved = jnp.where(over, here, 0.0)
    place = jnp.where(over, over_parts(here * held + moved * before(moved)), place)
    fits = place < POOL

    def turns(to_next, to_last):
        sent = jnp.where(part == 0, ones_where(there == to_next), ones_where(there == to_last))
        sent = jnp.where(mark == part + 1, jnp.where(fits, sent, 0.0), 0.0)
        count = jnp.broadcast_to(jnp.sum(sent, axis=1, keepdims=True), (PLANES * 8, LANE))
        row, col = iota((PLANES * 8, PLANES * 8), 0), iota((PLANES * 8, PLANES * 8), 1)
        sooner = ones_where(((col >> 3) < (row >> 3)) & ((col & 7) == (row & 7)))
        sooner = dot(sooner.astype(bf16), count.astype(bf16))[:, :1]
        return over_parts(sent) > 0, over_parts(sent * (before(sent) + sooner))

    passing, turn = turns(z, z)
    guest, seat = turns(z_peer(PLANES - 1), z_peer(1))
    late = ones_where(jnp.logical_not(fits)) + ones_where(passing & (turn >= PASS))
    late = jnp.max(jnp.max(late, axis=1, keepdims=True), axis=0, keepdims=True)

    row_code = ((ids & (ROWS - 1)) + 1).astype(jnp.float32)
    owner_code = (owner & (CHIPS * CORES - 1)).astype(jnp.float32)
    fields = jnp.where(part == 0, row_code, jnp.where(part == 1, owner_code, 0.0))
    fields = jnp.where(part == 2, mark.astype(jnp.float32), fields)
    fields = jnp.where(part == 3, turn.astype(jnp.float32), fields)
    entry = jnp.where((there == z) & fits, chip * POOL + place, -1)
    entry = jnp.where(guest & (seat < PASS), FIRST + (mark - 1) * PASS + seat, entry)
    got = jnp.zeros((8, ENTRIES), jnp.float32)
    for c in range(PLANES):
        where_at = ones_where(iota((ENTRIES, toks), 0) == entry[8 * c : 8 * c + 1])
        got = got + dot_nt(fields[8 * c : 8 * c + 8], where_at)
    mark = got[2:3, :FIRST].astype(jnp.int32)
    turn = got[3:4, :FIRST].astype(jnp.int32)
    pass_at = jnp.where((mark > 0) & (turn < PASS), (mark - 1) * PASS + turn, -1)
    taker = ones_where(iota((SPARE, FIRST), 0) == pass_at)
    staying = (iota((1, ENTRIES), 1) >= FIRST) | (got[2:3] < 0.5)
    entry_row = jnp.where(staying, got[0:1], 0.0)
    entry_owner = got[1:2].astype(jnp.int32)
    valid = entry_row > 0.0
    entry_chip = jnp.where(valid, entry_owner >> 1, -1)
    entry_core = (entry_owner & 1).astype(jnp.float32)
    place_in = ranks(entry_chip, CHIPS, ENTRIES)
    late = late + ones_where(jnp.max(place_in, axis=1, keepdims=True) >= PAIR)
    fits_in = valid & (place_in < PAIR)
    line = iota((CHIPS * 8, ENTRIES), 0)
    part_in = line & 7
    sent = jnp.where(part_in == 0, entry_row, jnp.where(part_in == 1, entry_core, 0.0))
    sent = jnp.where((line >> 3) == entry_chip, sent, 0.0)
    lanes = CHIPS // 2 * PAIR
    lane_at = jnp.where(fits_in, lax.rem(p, CHIPS // 2) * PAIR + place_in, -1)
    where_at = ones_where(iota((lanes, ENTRIES), 0) == lane_at)
    message = dot_nt(sent, where_at) + jnp.where(iota((CHIPS * 8, lanes), 0) & 7 == 2, late, 0.0)
    preq_send[...] = message.reshape(CHIPS, 8, lanes)
    p_start(preq_send, preq_recv, req_sem.at[5], req_sem.at[6], req_sem.at[7])

    slot = jnp.where(fits, there * POOL + place, -1)
    slot = jnp.sum(jnp.where(iota(shape, 0) == z * 8, slot, 0).astype(jnp.float32), axis=0, keepdims=True)
    packer = ones_where(iota((FIRST, toks), 0) == slot.astype(jnp.int32))
    pack[...] = packer.astype(bf16)

    def store(ref, k, matrix, rows):
        for h in range(2):
            cols = slice(h * half, (h + 1) * half)
            out = dot(matrix, rows[:, cols]).astype(bf16)
            ref[k, :, :, cols] = out.reshape(ref.shape[1], BLOCK, half)

    def pack_grads(k):
        own_in(grads_hbm, grads, 0, k).wait()
        mate_in(grads_hbm, grads, 0, k).wait_recv()
        store(z_send, k, pack[...], grads[k].reshape(toks, width))
        z_start(z_send.at[k], g1_recv.at[k], g1_sem.at[0, k], g1_sem.at[1, k], g1_sem.at[2, k], POOL // BLOCK)


    pack_grads(0)
    unpack[...] = packer.T.astype(bf16)
    take[...] = taker[: 2 * PASS].astype(bf16)
    spreader = ones_where(iota((SLOTS, ENTRIES), 0) == jnp.where(fits_in, entry_chip * PAIR + place_in, -1))
    spread[...] = spreader.astype(bf16)
    returned = [taker[PASS : 2 * PASS], taker[:PASS], taker[2 * PASS :]]
    unspread[...] = jnp.concatenate([spreader[:, :FIRST]] + returned, axis=0).T.astype(bf16)
    give[...] = spreader[:, FIRST:].T[: 2 * PASS].astype(bf16)

    wait_recv(preq_recv, CHIPS, req_sem.at[6], req_sem.at[7])
    got = preq_recv[...]
    got = jnp.concatenate([got[:8].sum(axis=0), got[8:].sum(axis=0)], axis=1)
    wanted = got[0:1] + got[1:2] * float(ROWS)
    adding = ones_where((iota((CORES * ROWS, SLOTS), 0) + 1).astype(jnp.float32) == wanted)
    adder[...] = adding.astype(bf16)
    pick[...] = adding.T.astype(bf16)
    late = jnp.sum(got[2:3], axis=1, keepdims=True)

    def pick_rows(k):
        own_in(table_hbm, table, 1, k).wait()
        mate_in(table_hbm, table, 2, k).wait_recv()
        store(p_send, k, pick[...], table[k].reshape(CORES * ROWS, width))
        p_start(p_send.at[k], e1_recv.at[k], e1_sem.at[0, k], e1_sem.at[1, k], e1_sem.at[2, k], PAIR // BLOCK)

    pick_rows(0)
    flag_send[...] = jnp.broadcast_to(late, flag_send.shape)
    z_start(flag_send, flag_recv, late_sem.at[0], late_sem.at[1], late_sem.at[2])

    def first_hop(k):
        pack_grads(k)
        pick_rows(k)

    loop(1, LEAD, first_hop)

    def on(k, side):
        return passed(on_send.at[k], g1_recv.at[k], lambda i: on_sem.at[i, k], z_blocks, side)

    def back(k, side):
        return passed(back_send.at[k], e1_recv.at[k], lambda i: back_sem.at[i, k], p_blocks, side)

    def pass_on(k):
        wait_recv(g1_recv.at[k], PLANES, g1_sem.at[1, k], g1_sem.at[2, k], POOL // BLOCK)
        rows = g1_recv[k, pl.ds(0, z_blocks)].reshape(FIRST, width)
        on_send[k] = dot(take[...], rows).astype(bf16).reshape(2, PASS, width)
        for side in range(2):
            on(k, side).start()
        wait_recv(e1_recv.at[k], CHIPS, e1_sem.at[1, k], e1_sem.at[2, k], PAIR // BLOCK)
        rows = e1_recv[k, pl.ds(0, p_blocks)].reshape(SLOTS, width)
        rows = dot(give[...], rows).astype(bf16).reshape(2, PASS, width)
        back_send[k, 0] = rows[1]
        back_send[k, 1] = rows[0]
        for side in range(2):
            back(k, side).start()

    def second_hop(k):
        wait_bytes(z_send.at[k], (PLANES - 1) * (POOL // BLOCK), g1_sem.at[0, k])
        for side in range(2):
            back(k, side).wait_recv()
        store(z_send, k, unspread[...], e1_recv[k].reshape(SLOTS + SPARE, width))
        z_start(z_send.at[k], e2_recv.at[k], e2_sem.at[0, k], e2_sem.at[1, k], e2_sem.at[2, k], POOL // BLOCK)
        wait_bytes(p_send.at[k], (CHIPS - 1) * (PAIR // BLOCK), e1_sem.at[0, k])
        for side in range(2):
            on(k, side).wait_recv()
        store(p_send, k, spread[...], g1_recv[k].reshape(ENTRIES, width))
        p_start(p_send.at[k], g2_recv.at[k], g2_sem.at[0, k], g2_sem.at[1, k], g2_sem.at[2, k], PAIR // BLOCK)

    def turn_round(k):
        pass_on(k)
        second_hop(k - 1)

    def whole_step(k):
        turn_round(k)
        first_hop(k + LEAD)

    pass_on(0)
    first_hop(LEAD)
    loop(1, CHUNKS - LEAD, whole_step)
    loop(CHUNKS - LEAD, CHUNKS, turn_round)
    second_hop(CHUNKS - 1)

    def own_out(vmem, hbm, i, k):
        return pltpu.make_async_copy(vmem.at[k, core], hbm.at[:, columns(core, k)], out_sem.at[i, k])

    def mate_out(vmem, hbm, i, k):
        return pltpu.make_async_remote_copy(
            src_ref=vmem.at[k, mate], dst_ref=hbm.at[:, columns(core, k)],
            send_sem=mate_sem.at[i, k], recv_sem=mate_sem.at[i + 1, k],
            device_id=device(z, p, mate), device_id_type=MESH,
        )

    def finish(k):
        wait_recv(e2_recv.at[k], PLANES, e2_sem.at[1, k], e2_sem.at[2, k], POOL // BLOCK)
        rows = e2_recv[k].reshape(FIRST, width)
        for h in range(2):
            cols = slice(h * half, (h + 1) * half)
            emb[k, :, :, cols] = dot(unpack[...], rows[:, cols]).astype(bf16).reshape(CORES, TOKS, half)
        mate_out(emb, emb_hbm, 4, k).start()
        own_out(emb, emb_hbm, 0, k).start()
        wait_recv(g2_recv.at[k], CHIPS, g2_sem.at[1, k], g2_sem.at[2, k], PAIR // BLOCK)
        rows = g2_recv[k].reshape(SLOTS, width)
        for h in range(2):
            cols = slice(h * half, (h + 1) * half)
            tgr[k, :, :, cols] = dot(adder[...], rows[:, cols]).astype(bf16).reshape(CORES, ROWS, half)
        mate_out(tgr, tgr_hbm, 6, k).start()
        own_out(tgr, tgr_hbm, 1, k).start()

    loop(0, CHUNKS, finish)
    wait_recv(flag_recv, PLANES, late_sem.at[1], late_sem.at[2])
    flag_ref[0, 0] = jnp.max(flag_recv[...])

    def drain(k):
        mate_in(grads_hbm, grads, 0, k).wait_send()
        mate_in(table_hbm, table, 2, k).wait_send()
        wait_bytes(z_send.at[k], (PLANES - 1) * (POOL // BLOCK), e2_sem.at[0, k])
        wait_bytes(p_send.at[k], (CHIPS - 1) * (PAIR // BLOCK), g2_sem.at[0, k])
        for side in range(2):
            on(k, side).wait_send()
            back(k, side).wait_send()
        own_out(emb, emb_hbm, 0, k).wait()
        own_out(tgr, tgr_hbm, 1, k).wait()
        mate_out(emb, emb_hbm, 4, k).wait()
        mate_out(tgr, tgr_hbm, 6, k).wait()

    loop(0, CHUNKS, drain)
    wait_bytes(line_recv, line_count - 1, req_sem.at[0])
    wait_bytes(preq_send, CHIPS - 1, req_sem.at[5])
    wait_bytes(flag_send, PLANES - 1, late_sem.at[0])


def routed(embedding_table, token_ids, output_grads):
    depth = embedding_table.shape[1]
    width = depth // (CORES * CHUNKS)
    bf16, f32 = jnp.bfloat16, jnp.float32
    anywhere = pl.BlockSpec(memory_space=pl.ANY)
    dma = pltpu.SemaphoreType.DMA
    toks, rows = CORES * TOKS, CORES * ROWS

    def blocks(count):
        return pltpu.VMEM((CHUNKS, count // BLOCK, BLOCK, width), bf16)

    row_block = pltpu.VMEM((CHUNKS, CORES, ROWS, width), bf16)
    tok_block = pltpu.VMEM((CHUNKS, CORES, TOKS, width), bf16)
    late_note = pltpu.VMEM((PLANES, 8, LANE), f32)
    p_note = pltpu.VMEM((CHIPS, 8, CHIPS // 2 * PAIR), f32)
    return pl.pallas_call(
        kernel,
        out_shape=(
            jax.ShapeDtypeStruct((TOKS, depth), bf16),
            jax.ShapeDtypeStruct((ROWS, depth), bf16),
            jax.ShapeDtypeStruct((1, 1), f32),
        ),
        in_specs=[pl.BlockSpec(memory_space=pltpu.VMEM), anywhere, anywhere],
        out_specs=(anywhere, anywhere, pl.BlockSpec(memory_space=pltpu.SMEM)),
        scratch_shapes=[
            row_block, tok_block, tok_block, row_block,
            blocks(FIRST), blocks(ENTRIES), blocks(FIRST),
            blocks(SLOTS), blocks(SLOTS + SPARE), blocks(SLOTS),
            blocks(2 * PASS), blocks(2 * PASS),
            pltpu.VMEM((8, TOKS), jnp.int32), pltpu.VMEM((PLANES * CORES, 8, TOKS), jnp.int32),
            p_note, p_note, late_note, late_note,
            pltpu.VMEM((FIRST, toks), bf16),
            pltpu.VMEM((toks, FIRST), bf16),
            pltpu.VMEM((SLOTS, ENTRIES), bf16),
            pltpu.VMEM((FIRST, SLOTS + SPARE), bf16),
            pltpu.VMEM((SLOTS, rows), bf16),
            pltpu.VMEM((rows, SLOTS), bf16),
            pltpu.VMEM((2 * PASS, FIRST), bf16),
            pltpu.VMEM((2 * PASS, SLOTS), bf16),
            dma((2, CHUNKS)),
            dma((2, CHUNKS)),
            dma((8, CHUNKS)),
            dma((3,)),
            dma((8,)),
            dma((3, CHUNKS)),
            dma((3, CHUNKS)),
            dma((3, CHUNKS)),
            dma((3, CHUNKS)),
            dma((4, CHUNKS)),
            dma((4, CHUNKS)),
        ],
        compiler_params=pltpu.CompilerParams(
            collective_id=0, has_side_effects=True, vmem_limit_bytes=56 * 1024 * 1024
        ),
    )(token_ids.reshape(1, TOKS), embedding_table, output_grads)


def on_device(embedding_table, token_ids, output_grads):
    embedded, table_grads, late = routed(embedding_table, token_ids, output_grads)

    def again(_):
        emb, tgr = general(embedding_table, token_ids, output_grads)
        return emb, tgr, jnp.float32(0)

    embedded, table_grads, _ = lax.while_loop(
        lambda held: held[2] > 0, again, (embedded, table_grads, late[0, 0])
    )
    return embedded, table_grads


def solution(mesh):
    return jax.shard_map(
        on_device,
        mesh=mesh,
        in_specs=(P("vocab", None), P("vocab"), P("vocab", None)),
        out_specs=(P("vocab", None), P("vocab", None)),
        check_vma=False,
    )
```

```python
import jax
import jax.numpy as jnp
from jax import lax
from jax.experimental import pallas as pl
from jax.experimental.pallas import tpu as pltpu
from jax.sharding import PartitionSpec as P

MESH = pl.DeviceIdType.MESH
PLANES = 8
CHIPS = 16
CORES = 2
ROWS = 256
TOKS = 128
LANE = 128
BLOCK = 16
POOL = 48
PASS = 16
PAIR = 48
CHUNKS = 8
LEAD = 3
FIRST = PLANES * POOL
SLOTS = CHIPS * PAIR
SPARE = LANE
ENTRIES = FIRST + SPARE


def ranks_within(owners):
    count = owners.shape[-1]
    earlier = lax.broadcasted_iota(jnp.int32, (count, count), 1) < lax.broadcasted_iota(
        jnp.int32, (count, count), 0
    )
    same = owners[..., :, None] == owners[..., None, :]
    return jnp.sum((same & earlier).astype(jnp.int32), axis=-1)


def general(embedding_table, token_ids, output_grads):
    row_count = embedding_table.shape[0]
    tok_count = token_ids.shape[0]
    width = embedding_table.shape[1]
    devices = lax.axis_size("vocab")
    capacity = 2 * ((tok_count + devices - 1) // devices)
    slots = devices * capacity
    owners = token_ids // row_count
    local_rows = token_ids - owners * row_count
    target = owners * capacity + ranks_within(owners)
    slot_column = lax.broadcasted_iota(jnp.int32, (slots, 1), 0)
    sender = target[None, :] == slot_column
    grad_buffer = jnp.dot(
        sender.astype(jnp.bfloat16), output_grads, preferred_element_type=jnp.float32
    )
    grad_buffer = grad_buffer.astype(jnp.bfloat16).reshape(devices, capacity, width)
    request = jnp.sum(sender.astype(jnp.int32) * (local_rows + 1)[None, :], axis=1)
    received = lax.all_to_all(
        request.reshape(devices, capacity), "vocab", split_axis=0, concat_axis=0, tiled=True
    )
    flat_rows = received.reshape(slots) - 1
    row_iota = lax.broadcasted_iota(jnp.int32, (1, row_count), 1)
    picker = (flat_rows[:, None] == row_iota).astype(jnp.bfloat16)
    picked = jnp.dot(picker, embedding_table, preferred_element_type=jnp.float32)
    picked = picked.astype(jnp.bfloat16).reshape(devices, capacity, width)
    returned = lax.all_to_all(picked, "vocab", split_axis=0, concat_axis=0, tiled=True)
    grads_in = lax.all_to_all(grad_buffer, "vocab", split_axis=0, concat_axis=0, tiled=True)
    slot_row = lax.broadcasted_iota(jnp.int32, (1, slots), 1)
    gatherer = (target[:, None] == slot_row).astype(jnp.bfloat16)
    embedded = jnp.dot(
        gatherer, returned.reshape(slots, width), preferred_element_type=jnp.float32
    ).astype(jnp.bfloat16)
    row_column = lax.broadcasted_iota(jnp.int32, (row_count, 1), 0)
    adder = (row_column == flat_rows[None, :]).astype(jnp.bfloat16)
    table_grads = jnp.dot(
        adder, grads_in.reshape(slots, width), preferred_element_type=jnp.float32
    ).astype(jnp.bfloat16)
    return embedded, table_grads


def iota(shape, axis):
    return lax.broadcasted_iota(jnp.int32, shape, axis)


def ones_where(mask):
    return jnp.where(mask, 1.0, 0.0)


def dot(a, b):
    return jnp.dot(a, b, preferred_element_type=jnp.float32)


def dot_nt(a, b):
    return lax.dot_general(
        a.astype(jnp.bfloat16),
        b.astype(jnp.bfloat16),
        (((1,), (1,)), ((), ())),
        preferred_element_type=jnp.float32,
    )


def kernel(
    ids_ref, table_hbm, grads_hbm, emb_hbm, tgr_hbm, flag_ref,
    table, grads, emb, tgr,
    z_send, g1_recv, e2_recv,
    p_send, e1_recv, g2_recv,
    on_send, back_send,
    ids_send, line_recv, preq_send, preq_recv, flag_send, flag_recv,
    pack, unpack, spread, unspread, pick, adder, take, give,
    in_sem, out_sem, mate_sem, late_sem, req_sem,
    g1_sem, e1_sem, g2_sem, e2_sem, on_sem, back_sem,
):
    me = lax.axis_index("vocab")
    core = lax.rem(me, CORES)
    mate = 1 - core
    z = me // (CHIPS * CORES)
    p = lax.rem(me // CORES, CHIPS)
    width = table.shape[3]
    half = width // 2
    bf16 = jnp.bfloat16
    z_blocks, p_blocks = FIRST // BLOCK, SLOTS // BLOCK

    def device(plane, chip, which):
        return ((plane * CHIPS + chip) * CORES + which,)

    def z_peer(j):
        return lax.rem(z + j, PLANES)

    def p_peer(j):
        return lax.rem(p + j, CHIPS)

    def loop(lo, hi, body):
        def step(j, carry):
            body(j)
            return carry

        lax.fori_loop(lo, hi, step, 0)

    def columns(which, k):
        return pl.ds(pl.multiple_of((which * CHUNKS + k) * width, width), width)

    barrier = pltpu.get_barrier_semaphore()

    def greet(plane, chip, which):
        pl.semaphore_signal(barrier, inc=1, device_id=device(plane, chip, which), device_id_type=MESH)

    line_count = PLANES * CORES
    line_me = z * CORES + core

    def line_peer(j):
        return lax.rem(line_me + j, line_count)

    loop(1, line_count, lambda j: greet(line_peer(j) // CORES, p, lax.rem(line_peer(j), CORES)))
    loop(1, CHIPS, lambda j: greet(z, p_peer(j), core))

    def own_in(hbm, vmem, i, k):
        return pltpu.make_async_copy(hbm.at[:, columns(core, k)], vmem.at[k, core], in_sem.at[i, k])

    def mate_in(hbm, vmem, i, k):
        return pltpu.make_async_remote_copy(
            src_ref=hbm.at[:, columns(mate, k)], dst_ref=vmem.at[k, core],
            send_sem=mate_sem.at[i, k], recv_sem=mate_sem.at[i + 1, k],
            device_id=device(z, p, mate), device_id_type=MESH,
        )

    loop(0, CHUNKS, lambda k: own_in(grads_hbm, grads, 0, k).start())
    loop(0, CHUNKS, lambda k: own_in(table_hbm, table, 1, k).start())

    def clear(k):
        first = z_blocks + 2
        count = SPARE // BLOCK - 2
        g1_recv[k, pl.ds(first, count)] = jnp.zeros((count, BLOCK, width), bf16)
        first = p_blocks + 2
        e1_recv[k, pl.ds(first, count)] = jnp.zeros((count, BLOCK, width), bf16)

    loop(0, CHUNKS, clear)

    def z_start(src, dst, send, recv, own, count=1):
        def at(ref, t):
            return ref.at[pl.ds(t * count, count)]

        def one(j):
            t = z_peer(j)
            pltpu.make_async_remote_copy(
                src_ref=at(src, t), dst_ref=at(dst, z), send_sem=send, recv_sem=recv,
                device_id=device(t, p, core), device_id_type=MESH,
            ).start()

        loop(1, PLANES, one)
        pltpu.make_async_copy(at(src, z), at(dst, z), own).start()

    def p_start(src, dst, send, recv, own, count=1):
        def at(ref, t):
            return ref.at[pl.ds(t * count, count)]

        def one(j):
            t = p_peer(j)
            pltpu.make_async_remote_copy(
                src_ref=at(src, t), dst_ref=at(dst, p), send_sem=send, recv_sem=recv,
                device_id=device(z, t, core), device_id_type=MESH,
            ).start()

        loop(1, CHIPS, one)
        pltpu.make_async_copy(at(src, p), at(dst, p), own).start()

    def passed(src, dst, sem, first, side):
        t = lax.rem(z + (1 if side == 0 else PLANES - 1), PLANES)
        return pltpu.make_async_remote_copy(
            src_ref=src.at[side], dst_ref=dst.at[first + side],
            send_sem=sem(side), recv_sem=sem(2 + side),
            device_id=device(t, p, core), device_id_type=MESH,
        )

    def wait_bytes(ref, count, sem):
        pltpu.make_async_copy(ref.at[pl.ds(0, count)], ref.at[pl.ds(0, count)], sem).wait()

    def wait_recv(dst, peers, recv, own, count=1):
        wait_bytes(dst, (peers - 1) * count, recv)
        wait_bytes(dst, count, own)

    ids_send[...] = jnp.broadcast_to(ids_ref[...], ids_send.shape)
    line_recv[line_me] = ids_send[...]
    pl.semaphore_wait(barrier, line_count - 1 + CHIPS - 1)

    def ids_copy(j):
        t = line_peer(j)
        return pltpu.make_async_remote_copy(
            src_ref=ids_send, dst_ref=line_recv.at[line_me],
            send_sem=req_sem.at[0], recv_sem=req_sem.at[1],
            device_id=device(t // CORES, p, lax.rem(t, CORES)), device_id_type=MESH,
        )

    loop(1, line_count, lambda j: ids_copy(j).start())
    loop(0, CHUNKS, lambda k: mate_in(grads_hbm, grads, 0, k).start())
    loop(0, CHUNKS, lambda k: mate_in(table_hbm, table, 2, k).start())
    wait_bytes(line_recv, line_count - 1, req_sem.at[1])
    toks = CORES * TOKS
    got = line_recv[...].reshape(PLANES, CORES, 8, TOKS)
    ids = jnp.concatenate([got[:, c].reshape(PLANES * 8, TOKS) for c in range(CORES)], axis=1)

    def ranks(keys, kinds, count):
        same = ones_where(iota((kinds, count), 0) == keys)
        earlier = ones_where(iota((count, count), 0) < iota((count, count), 1))
        before = dot(same.astype(bf16), earlier.astype(bf16))
        return jnp.sum(same * before, axis=0, keepdims=True).astype(jnp.int32)

    shape = (PLANES * 8, toks)
    chip = iota(shape, 0) >> 3
    part = iota(shape, 0) & 7
    earlier = ones_where(iota((toks, toks), 0) < iota((toks, toks), 1)).astype(bf16)

    def before(mask):
        return dot(mask.astype(bf16), earlier)

    def over_parts(x):
        x = jnp.sum(x.reshape(PLANES, 8, toks), axis=1, keepdims=True)
        return jnp.broadcast_to(x, (PLANES, 8, toks)).reshape(shape).astype(jnp.int32)

    plane = lax.shift_right_logical(ids, 13)
    owner = lax.shift_right_logical(ids, 8)
    same = ones_where(plane == part)
    place = over_parts(same * before(same))
    over = place >= POOL
    ahead = (plane - chip + PLANES) & (PLANES - 1)
    up = (ahead >= 1) & (ahead <= PLANES // 2)
    mark = jnp.where(over, jnp.where(up, 1, 2), 0)
    there = (plane + jnp.where(over, jnp.where(up, PLANES - 1, 1), 0)) & (PLANES - 1)
    held = jnp.minimum(jnp.sum(same, axis=1, keepdims=True), float(POOL))
    here = ones_where(there == part)
    moved = jnp.where(over, here, 0.0)
    place = jnp.where(over, over_parts(here * held + moved * before(moved)), place)
    fits = place < POOL

    def turns(to_next, to_last):
        sent = jnp.where(part == 0, ones_where(there == to_next), ones_where(there == to_last))
        sent = jnp.where(mark == part + 1, jnp.where(fits, sent, 0.0), 0.0)
        count = jnp.broadcast_to(jnp.sum(sent, axis=1, keepdims=True), (PLANES * 8, LANE))
        row, col = iota((PLANES * 8, PLANES * 8), 0), iota((PLANES * 8, PLANES * 8), 1)
        sooner = ones_where(((col >> 3) < (row >> 3)) & ((col & 7) == (row & 7)))
        sooner = dot(sooner.astype(bf16), count.astype(bf16))[:, :1]
        return over_parts(sent) > 0, over_parts(sent * (before(sent) + sooner))

    passing, turn = turns(z, z)
    guest, seat = turns(z_peer(PLANES - 1), z_peer(1))
    late = ones_where(jnp.logical_not(fits)) + ones_where(passing & (turn >= PASS))
    late = jnp.max(jnp.max(late, axis=1, keepdims=True), axis=0, keepdims=True)

    row_code = ((ids & (ROWS - 1)) + 1).astype(jnp.float32)
    owner_code = (owner & (CHIPS * CORES - 1)).astype(jnp.float32)
    fields = jnp.where(part == 0, row_code, jnp.where(part == 1, owner_code, 0.0))
    fields = jnp.where(part == 2, mark.astype(jnp.float32), fields)
    fields = jnp.where(part == 3, turn.astype(jnp.float32), fields)
    entry = jnp.where((there == z) & fits, chip * POOL + place, -1)
    entry = jnp.where(guest & (seat < PASS), FIRST + (mark - 1) * PASS + seat, entry)
    got = jnp.zeros((8, ENTRIES), jnp.float32)
    for c in range(PLANES):
        where_at = ones_where(iota((ENTRIES, toks), 0) == entry[8 * c : 8 * c + 1])
        got = got + dot_nt(fields[8 * c : 8 * c + 8], where_at)
    mark = got[2:3, :FIRST].astype(jnp.int32)
    turn = got[3:4, :FIRST].astype(jnp.int32)
    pass_at = jnp.where((mark > 0) & (turn < PASS), (mark - 1) * PASS + turn, -1)
    taker = ones_where(iota((SPARE, FIRST), 0) == pass_at)
    staying = (iota((1, ENTRIES), 1) >= FIRST) | (got[2:3] < 0.5)
    entry_row = jnp.where(staying, got[0:1], 0.0)
    entry_owner = got[1:2].astype(jnp.int32)
    valid = entry_row > 0.0
    entry_chip = jnp.where(valid, entry_owner >> 1, -1)
    entry_core = (entry_owner & 1).astype(jnp.float32)
    place_in = ranks(entry_chip, CHIPS, ENTRIES)
    late = late + ones_where(jnp.max(place_in, axis=1, keepdims=True) >= PAIR)
    fits_in = valid & (place_in < PAIR)
    line = iota((CHIPS * 8, ENTRIES), 0)
    part_in = line & 7
    sent = jnp.where(part_in == 0, entry_row, jnp.where(part_in == 1, entry_core, 0.0))
    sent = jnp.where((line >> 3) == entry_chip, sent, 0.0)
    lanes = CHIPS // 2 * PAIR
    lane_at = jnp.where(fits_in, lax.rem(p, CHIPS // 2) * PAIR + place_in, -1)
    where_at = ones_where(iota((lanes, ENTRIES), 0) == lane_at)
    message = dot_nt(sent, where_at) + jnp.where(iota((CHIPS * 8, lanes), 0) & 7 == 2, late, 0.0)
    preq_send[...] = message.reshape(CHIPS, 8, lanes)
    p_start(preq_send, preq_recv, req_sem.at[5], req_sem.at[6], req_sem.at[7])

    slot = jnp.where(fits, there * POOL + place, -1)
    slot = jnp.sum(jnp.where(iota(shape, 0) == z * 8, slot, 0).astype(jnp.float32), axis=0, keepdims=True)
    packer = ones_where(iota((FIRST, toks), 0) == slot.astype(jnp.int32))
    pack[...] = packer.astype(bf16)

    def store(ref, k, matrix, rows):
        for h in range(2):
            cols = slice(h * half, (h + 1) * half)
            out = dot(matrix, rows[:, cols]).astype(bf16)
            ref[k, :, :, cols] = out.reshape(ref.shape[1], BLOCK, half)

    def pack_grads(k):
        own_in(grads_hbm, grads, 0, k).wait()
        mate_in(grads_hbm, grads, 0, k).wait_recv()
        store(z_send, k, pack[...], grads[k].reshape(toks, width))
        z_start(z_send.at[k], g1_recv.at[k], g1_sem.at[0, k], g1_sem.at[1, k], g1_sem.at[2, k], POOL // BLOCK)


    pack_grads(0)
    unpack[...] = packer.T.astype(bf16)
    take[...] = taker[: 2 * PASS].astype(bf16)
    spreader = ones_where(iota((SLOTS, ENTRIES), 0) == jnp.where(fits_in, entry_chip * PAIR + place_in, -1))
    spread[...] = spreader.astype(bf16)
    returned = [taker[PASS : 2 * PASS], taker[:PASS], taker[2 * PASS :]]
    unspread[...] = jnp.concatenate([spreader[:, :FIRST]] + returned, axis=0).T.astype(bf16)
    give[...] = spreader[:, FIRST:].T[: 2 * PASS].astype(bf16)

    wait_recv(preq_recv, CHIPS, req_sem.at[6], req_sem.at[7])
    got = preq_recv[...]
    got = jnp.concatenate([got[:8].sum(axis=0), got[8:].sum(axis=0)], axis=1)
    wanted = got[0:1] + got[1:2] * float(ROWS)
    adding = ones_where((iota((CORES * ROWS, SLOTS), 0) + 1).astype(jnp.float32) == wanted)
    adder[...] = adding.astype(bf16)
    pick[...] = adding.T.astype(bf16)
    late = jnp.sum(got[2:3], axis=1, keepdims=True)

    def pick_rows(k):
        own_in(table_hbm, table, 1, k).wait()
        mate_in(table_hbm, table, 2, k).wait_recv()
        store(p_send, k, pick[...], table[k].reshape(CORES * ROWS, width))
        p_start(p_send.at[k], e1_recv.at[k], e1_sem.at[0, k], e1_sem.at[1, k], e1_sem.at[2, k], PAIR // BLOCK)

    pick_rows(0)
    flag_send[...] = jnp.broadcast_to(late, flag_send.shape)
    z_start(flag_send, flag_recv, late_sem.at[0], late_sem.at[1], late_sem.at[2])

    def first_hop(k):
        pack_grads(k)
        pick_rows(k)

    loop(1, LEAD, first_hop)

    def on(k, side):
        return passed(on_send.at[k], g1_recv.at[k], lambda i: on_sem.at[i, k], z_blocks, side)

    def back(k, side):
        return passed(back_send.at[k], e1_recv.at[k], lambda i: back_sem.at[i, k], p_blocks, side)

    def pass_on(k):
        wait_recv(g1_recv.at[k], PLANES, g1_sem.at[1, k], g1_sem.at[2, k], POOL // BLOCK)
        rows = g1_recv[k, pl.ds(0, z_blocks)].reshape(FIRST, width)
        on_send[k] = dot(take[...], rows).astype(bf16).reshape(2, PASS, width)
        for side in range(2):
            on(k, side).start()
        wait_recv(e1_recv.at[k], CHIPS, e1_sem.at[1, k], e1_sem.at[2, k], PAIR // BLOCK)
        rows = e1_recv[k, pl.ds(0, p_blocks)].reshape(SLOTS, width)
        rows = dot(give[...], rows).astype(bf16).reshape(2, PASS, width)
        back_send[k, 0] = rows[1]
        back_send[k, 1] = rows[0]
        for side in range(2):
            back(k, side).start()

    def second_hop(k):
        wait_bytes(p_send.at[k], (CHIPS - 1) * (PAIR // BLOCK), e1_sem.at[0, k])
        for side in range(2):
            on(k, side).wait_recv()
        store(p_send, k, spread[...], g1_recv[k].reshape(ENTRIES, width))
        p_start(p_send.at[k], g2_recv.at[k], g2_sem.at[0, k], g2_sem.at[1, k], g2_sem.at[2, k], PAIR // BLOCK)
        wait_bytes(z_send.at[k], (PLANES - 1) * (POOL // BLOCK), g1_sem.at[0, k])
        for side in range(2):
            back(k, side).wait_recv()
        store(z_send, k, unspread[...], e1_recv[k].reshape(SLOTS + SPARE, width))
        z_start(z_send.at[k], e2_recv.at[k], e2_sem.at[0, k], e2_sem.at[1, k], e2_sem.at[2, k], POOL // BLOCK)

    def own_out(vmem, hbm, i, k):
        return pltpu.make_async_copy(vmem.at[k, core], hbm.at[:, columns(core, k)], out_sem.at[i, k])

    def mate_out(vmem, hbm, i, k):
        return pltpu.make_async_remote_copy(
            src_ref=vmem.at[k, mate], dst_ref=hbm.at[:, columns(core, k)],
            send_sem=mate_sem.at[i, k], recv_sem=mate_sem.at[i + 1, k],
            device_id=device(z, p, mate), device_id_type=MESH,
        )

    def finish(k):
        wait_recv(e2_recv.at[k], PLANES, e2_sem.at[1, k], e2_sem.at[2, k], POOL // BLOCK)
        rows = e2_recv[k].reshape(FIRST, width)
        for h in range(2):
            cols = slice(h * half, (h + 1) * half)
            emb[k, :, :, cols] = dot(unpack[...], rows[:, cols]).astype(bf16).reshape(CORES, TOKS, half)
        mate_out(emb, emb_hbm, 4, k).start()
        own_out(emb, emb_hbm, 0, k).start()
        wait_recv(g2_recv.at[k], CHIPS, g2_sem.at[1, k], g2_sem.at[2, k], PAIR // BLOCK)
        rows = g2_recv[k].reshape(SLOTS, width)
        for h in range(2):
            cols = slice(h * half, (h + 1) * half)
            tgr[k, :, :, cols] = dot(adder[...], rows[:, cols]).astype(bf16).reshape(CORES, ROWS, half)
        mate_out(tgr, tgr_hbm, 6, k).start()
        own_out(tgr, tgr_hbm, 1, k).start()

    def turn_round(k):
        pass_on(k)
        second_hop(k - 1)

    def whole_step(k):
        turn_round(k)
        first_hop(k + LEAD)

    pass_on(0)
    first_hop(LEAD)
    loop(1, CHUNKS - LEAD, whole_step)
    done = 2

    def late_step(k):
        turn_round(k)
        finish(k - (CHUNKS - done))

    loop(CHUNKS - LEAD, CHUNKS - done, turn_round)
    loop(CHUNKS - done, CHUNKS, late_step)
    second_hop(CHUNKS - 1)
    loop(done, CHUNKS, finish)

    wait_recv(flag_recv, PLANES, late_sem.at[1], late_sem.at[2])
    flag_ref[0, 0] = jnp.max(flag_recv[...])

    def drain(k):
        mate_in(grads_hbm, grads, 0, k).wait_send()
        mate_in(table_hbm, table, 2, k).wait_send()
        wait_bytes(z_send.at[k], (PLANES - 1) * (POOL // BLOCK), e2_sem.at[0, k])
        wait_bytes(p_send.at[k], (CHIPS - 1) * (PAIR // BLOCK), g2_sem.at[0, k])
        for side in range(2):
            on(k, side).wait_send()
            back(k, side).wait_send()
        own_out(emb, emb_hbm, 0, k).wait()
        own_out(tgr, tgr_hbm, 1, k).wait()
        mate_out(emb, emb_hbm, 4, k).wait()
        mate_out(tgr, tgr_hbm, 6, k).wait()

    loop(0, CHUNKS, drain)
    wait_bytes(line_recv, line_count - 1, req_sem.at[0])
    wait_bytes(preq_send, CHIPS - 1, req_sem.at[5])
    wait_bytes(flag_send, PLANES - 1, late_sem.at[0])


def routed(embedding_table, token_ids, output_grads):
    depth = embedding_table.shape[1]
    width = depth // (CORES * CHUNKS)
    bf16, f32 = jnp.bfloat16, jnp.float32
    anywhere = pl.BlockSpec(memory_space=pl.ANY)
    dma = pltpu.SemaphoreType.DMA
    toks, rows = CORES * TOKS, CORES * ROWS

    def blocks(count):
        return pltpu.VMEM((CHUNKS, count // BLOCK, BLOCK, width), bf16)

    row_block = pltpu.VMEM((CHUNKS, CORES, ROWS, width), bf16)
    tok_block = pltpu.VMEM((CHUNKS, CORES, TOKS, width), bf16)
    late_note = pltpu.VMEM((PLANES, 8, LANE), f32)
    p_note = pltpu.VMEM((CHIPS, 8, CHIPS // 2 * PAIR), f32)
    return pl.pallas_call(
        kernel,
        out_shape=(
            jax.ShapeDtypeStruct((TOKS, depth), bf16),
            jax.ShapeDtypeStruct((ROWS, depth), bf16),
            jax.ShapeDtypeStruct((1, 1), f32),
        ),
        in_specs=[pl.BlockSpec(memory_space=pltpu.VMEM), anywhere, anywhere],
        out_specs=(anywhere, anywhere, pl.BlockSpec(memory_space=pltpu.SMEM)),
        scratch_shapes=[
            row_block, tok_block, tok_block, row_block,
            blocks(FIRST), blocks(ENTRIES), blocks(FIRST),
            blocks(SLOTS), blocks(SLOTS + SPARE), blocks(SLOTS),
            blocks(2 * PASS), blocks(2 * PASS),
            pltpu.VMEM((8, TOKS), jnp.int32), pltpu.VMEM((PLANES * CORES, 8, TOKS), jnp.int32),
            p_note, p_note, late_note, late_note,
            pltpu.VMEM((FIRST, toks), bf16),
            pltpu.VMEM((toks, FIRST), bf16),
            pltpu.VMEM((SLOTS, ENTRIES), bf16),
            pltpu.VMEM((FIRST, SLOTS + SPARE), bf16),
            pltpu.VMEM((SLOTS, rows), bf16),
            pltpu.VMEM((rows, SLOTS), bf16),
            pltpu.VMEM((2 * PASS, FIRST), bf16),
            pltpu.VMEM((2 * PASS, SLOTS), bf16),
            dma((2, CHUNKS)),
            dma((2, CHUNKS)),
            dma((8, CHUNKS)),
            dma((3,)),
            dma((8,)),
            dma((3, CHUNKS)),
            dma((3, CHUNKS)),
            dma((3, CHUNKS)),
            dma((3, CHUNKS)),
            dma((4, CHUNKS)),
            dma((4, CHUNKS)),
        ],
        compiler_params=pltpu.CompilerParams(
            collective_id=0, has_side_effects=True, vmem_limit_bytes=56 * 1024 * 1024
        ),
    )(token_ids.reshape(1, TOKS), embedding_table, output_grads)


def on_device(embedding_table, token_ids, output_grads):
    embedded, table_grads, late = routed(embedding_table, token_ids, output_grads)

    def again(_):
        emb, tgr = general(embedding_table, token_ids, output_grads)
        return emb, tgr, jnp.float32(0)

    embedded, table_grads, _ = lax.while_loop(
        lambda held: held[2] > 0, again, (embedded, table_grads, late[0, 0])
    )
    return embedded, table_grads


def solution(mesh):
    return jax.shard_map(
        on_device,
        mesh=mesh,
        in_specs=(P("vocab", None), P("vocab"), P("vocab", None)),
        out_specs=(P("vocab", None), P("vocab", None)),
        check_vma=False,
    )
```
